32 devices in a mesh: group: 2 (over x), dp: 8 (over z, y), tensor: 2 (over core).
Axes of the slice: x: 2, y: 2, z: 4, core: 2. Of those that a mesh axis runs over, the one named last changes fastest.
Arguments:
- patch_feats: bfloat16 [6144, 3200], P(('group', 'dp')), parts along dimension 0, may hold values from -80 to 80
- ln_gain: float32 [12800], replicated, may hold values from 0.1 to 1.9
- ln_shift: float32 [12800], replicated, may hold values from -3 to 3
- merge_weight: bfloat16 [12800, 4096], P('dp', 'tensor'), may hold values from -0.0546875 to 0.0546875
- merge_bias: float32 [4096], P('tensor'), may hold values from -3 to 3
- tile_count: int32 [16], P('group'), parts along dimension 0, may hold values from 1 to 3
- tile_dest: int32 [48], P('group'), parts along dimension 0, may hold values from 0 to 23, each once
Outputs:
- placed: bfloat16 [1536, 4096], P(('group', 'dp'), 'tensor'), parts along dimension 0
The draws below stay inside these ranges and needn't reach their ends.
There are 2 independent parts, one for each index of `group`. The reference program is written for one: setup_inputs(seed, part) draws one part's arguments, and reference() takes and returns one part's arrays. A program takes and returns all parts, laid end to end along the dimension named above; an argument that names none is the same for every part. Nothing has to cross between parts.
Inputs may be any that keep to these rules, and one draw needn't show every extreme that they name: A device's tiles of 128 patch rows after its first tile_count tiles are padding. `tile_dest`: every output tile slot is named by exactly one tile.
All inputs are finite; a program needn't handle non-finite values.
Results may differ from the reference program's by a relative error of at most 0.013.
Values may be sent and summed in bfloat16 or wider, within the bound.
No kernel may reach another device: no remote copies, remote signals or barrier semaphores. Data moves between devices by JAX's collectives and lax.ppermute only.
A program may use at most 64 MiB of HBM per device.

```python
import math
import jax
import jax.numpy as jnp
from jax import lax

D = 3200
OUT = 4096
TILE = 128
MERGED = 12800
RM = 96
TILES = 3
PATCHES = 3072
MROWS = 768
SLOTS = 24
N_DP = 8


def draw_patch_feats(key, part):
    key = jax.random.fold_in(key, 11)
    key_entry, key_row, key_column = jax.random.split(key, 3)
    shape = (PATCHES, D)
    entries = jnp.clip(jax.random.normal(key_entry, shape, jnp.float32), -4.0, 4.0)
    row_scale = jnp.exp(jax.random.uniform(key_row, (PATCHES, 1), jnp.float32, 0.0, math.log(10.0)))
    column_scale = jnp.exp(jax.random.uniform(key_column, (1, D), jnp.float32, math.log(0.5), math.log(2.0)))
    return (entries * row_scale * column_scale).astype(jnp.bfloat16)


def set_ends(result, rng, low, largest):
    spot = [jax.random.randint(jax.random.fold_in(rng, axis), (), 0, length) for axis, length in enumerate(result.shape)]
    longest = result.shape.index(max(result.shape))
    next_to = spot[:longest] + [(spot[longest] + 1) % result.shape[longest]] + spot[longest + 1:]
    return result.at[tuple(spot)].set(low).at[tuple(next_to)].set(largest)


def steps_of(own_key, dims, shards, least, largest):
    def one(axis_at, shards_of):
        steps = jax.random.uniform(jax.random.fold_in(jax.random.fold_in(own_key, 6), axis_at), (shards_of,), jnp.float32, least / len(shards), largest / len(shards))
        return jnp.repeat(jnp.exp(steps), dims[axis_at] // shards_of).reshape((-1,) + (1,) * (len(dims) - axis_at - 1))

    gain = one(*shards[0])
    for cut in shards[1:]:
        gain = gain * one(*cut)
    return gain


def bell_draw(own_key, extent, scale, most, cuts=(), kind=jnp.bfloat16):
    result = jax.random.normal(own_key, extent, jnp.float32) * scale
    if len(cuts) > 0:
        result = steps_of(own_key, extent, cuts, -0.22, 0.18) * result
    return jnp.clip(result, min=-most, max=most).astype(kind)


def setup_inputs(seed: int = 0, part: int = 0) -> dict:
    arg_keys = jax.random.split(jax.random.key(seed), 8)
    own_keys = jax.random.split(jax.random.fold_in(arg_keys[7], part), 8)
    return {
        "patch_feats": draw_patch_feats(jax.random.fold_in(jax.random.fold_in(arg_keys[7], part), 71), part),
        "ln_gain": jnp.clip(1.0 + 0.18 * jax.random.normal(arg_keys[1], (MERGED,), jnp.float32), 0.1, 1.9),
        "ln_shift": bell_draw(arg_keys[2], (MERGED,), 0.5, 3.0, (), jnp.float32),
        "merge_weight": bell_draw(arg_keys[3], (MERGED, OUT), MERGED ** -0.5, 0.0546875, ((0, 8), (1, 2))),
        "merge_bias": bell_draw(arg_keys[4], (OUT,), 0.5, 3.0, ((0, 2),), jnp.float32),
        "tile_count": set_ends(jax.random.randint(own_keys[5], (N_DP,), 1, TILES + 1), jax.random.fold_in(own_keys[5], 1), 1, TILES).astype(jnp.int32),
        "tile_dest": jax.random.permutation(own_keys[6], SLOTS).astype(jnp.int32),
    }


def layer_norm(row_block, ln_gain, ln_shift):
    row_mean = lax.optimization_barrier(jnp.mean(row_block, axis=1, keepdims=True))
    centred = row_block - row_mean
    variance = lax.optimization_barrier(jnp.mean(centred * centred, axis=1, keepdims=True))
    return centred * lax.rsqrt(variance + 1e-06) * ln_gain + ln_shift

def reference(patch_feats, ln_gain, ln_shift, merge_weight, merge_bias, tile_count, tile_dest):
    merged = patch_feats.reshape(MROWS, MERGED).astype(jnp.float32)
    row_ids = jnp.arange(MROWS, dtype=jnp.int32)
    row_live = row_ids % RM // (TILE // 4) < tile_count[row_ids // RM]
    normed = jnp.where(row_live[:, None], layer_norm(merged, ln_gain, ln_shift), 0.0).astype(jnp.bfloat16)
    block_width = MERGED // N_DP

    def add_block(summed, block_index):
        first = (block_index * block_width).astype(jnp.int32)
        column_block = lax.dynamic_slice_in_dim(normed, first, block_width, 1)
        weight_block = lax.dynamic_slice_in_dim(merge_weight, first, block_width, 0)
        partial_value = jnp.dot(column_block, weight_block, preferred_element_type=jnp.float32).astype(jnp.bfloat16)
        partial_value = lax.optimization_barrier(partial_value)
        return (summed + partial_value.astype(jnp.float32), None)
    summed, unused = lax.scan(add_block, jnp.zeros((MROWS, OUT), jnp.float32), jnp.arange(N_DP, dtype=jnp.int32))
    activated = jax.nn.gelu(summed + merge_bias, approximate=False)
    projected = jnp.where(row_live[:, None], activated, 0.0).astype(jnp.bfloat16)
    tile_blocks = projected.reshape(SLOTS, TILE // 4, OUT)
    anchor = jnp.zeros((SLOTS,), jnp.int32).at[tile_dest].set(jnp.arange(SLOTS, dtype=jnp.int32))
    return tile_blocks[anchor].reshape(MROWS, OUT)
```

```python
import functools

import jax
import jax.numpy as jnp
from jax import lax
from jax.experimental import pallas as pl
from jax.experimental.pallas import tpu as pltpu
from jax.sharding import PartitionSpec as P

TILE = 128
TILE_ROWS = TILE // 4
HALF = TILE_ROWS // 2
VMEM_LIMIT = 40 * 1024 * 1024


def vmem():
    return pl.BlockSpec(memory_space=pltpu.VMEM)


def arrangement(bits):
    if not bits:
        return [0]
    rest = arrangement(bits[1:])
    return [owner ^ (1 << bits[0]) for owner in rest] + rest


def prepare_kernel(peers, tiles, scalars, x_ref, gain_ref, shift_ref, *refs):
    outs, pieces = refs[:-1], refs[-1]
    me, count = scalars[0], scalars[2]
    rows = tiles * HALF
    width = x_ref.shape[-1]
    total = 4 * width
    block_width = total // peers
    x = x_ref[...].reshape(4 * rows, width)
    row_out = lax.broadcasted_iota(jnp.int32, (4 * rows, 4 * rows), 0)
    row_in = lax.broadcasted_iota(jnp.int32, (4 * rows, 4 * rows), 1)
    quarter = jnp.zeros_like(row_out)
    for q in range(1, 4):
        quarter += (row_out >= q * rows).astype(jnp.int32)
    source = 4 * (row_out - quarter * rows) + quarter
    mix = (row_in == source).astype(jnp.bfloat16)
    y = jnp.dot(mix, x, preferred_element_type=jnp.float32)
    parts = [y[q * rows:(q + 1) * rows] for q in range(4)]
    mean = sum(jnp.sum(part, axis=1, keepdims=True) for part in parts) / total
    parts = [part - mean for part in parts]
    variance = sum(jnp.sum(part * part, axis=1, keepdims=True) for part in parts) / total
    scale = lax.rsqrt(variance + 1e-06)
    tile_of = lax.broadcasted_iota(jnp.int32, (rows, 1), 0) // HALF
    live = tile_of < count
    per_patch = width // block_width
    for q in range(4):
        normed = parts[q] * scale * gain_ref[pl.ds(q, 1), :] + shift_ref[pl.ds(q, 1), :]
        normed = jnp.where(live, normed, 0.0).astype(jnp.bfloat16)
        for part in range(per_patch):
            pieces[q * per_patch + part] = normed[:, part * block_width:(part + 1) * block_width]
    for k in range(peers):
        outs[k][...] = pieces[jnp.bitwise_xor(me, k)]


def prepare(scalars, patch_feats, ln_gain, ln_shift, peers, tiles):
    width = patch_feats.shape[1]
    block_width = 4 * width // peers
    rows = tiles * HALF
    x = patch_feats.reshape(tiles, 2, TILE // 2, width)
    piece = jax.ShapeDtypeStruct((rows, block_width), jnp.bfloat16)
    return pl.pallas_call(
        functools.partial(prepare_kernel, peers, tiles),
        grid_spec=pltpu.PrefetchScalarGridSpec(
            num_scalar_prefetch=1,
            grid=(1,),
            in_specs=[
                pl.BlockSpec((tiles, 1, TILE // 2, width), lambda i, s: (0, s[1], 0, 0)),
                pl.BlockSpec((4, width), lambda i, s: (0, 0)),
                pl.BlockSpec((4, width), lambda i, s: (0, 0)),
            ],
            out_specs=[pl.BlockSpec((rows, block_width), lambda i, s: (0, 0))] * peers,
            scratch_shapes=[pltpu.VMEM((peers, rows, block_width), jnp.bfloat16)],
        ),
        out_shape=[piece] * peers,
        compiler_params=pltpu.CompilerParams(vmem_limit_bytes=VMEM_LIMIT),
        name="prepare",
    )(scalars, x, ln_gain.reshape(4, width), ln_shift.reshape(4, width))


def gather_kernel(peers, order_ref, *refs):
    ins, out, held = refs[:peers], refs[peers], refs[peers + 1]
    rows = ins[0].shape[0]
    for k in range(peers):
        held[pl.ds(k * rows, rows), :] = ins[k][...]
    for i in range(peers * rows // HALF):
        first = pl.multiple_of(order_ref[i] * HALF, HALF)
        out[pl.ds(i * HALF, HALF), :] = held[pl.ds(first, HALF), :]


def gather_tiles(order, received):
    peers = len(received)
    rows, block_width = received[0].shape
    return pl.pallas_call(
        functools.partial(gather_kernel, peers),
        grid_spec=pltpu.PrefetchScalarGridSpec(
            num_scalar_prefetch=1,
            grid=(1,),
            in_specs=[pl.BlockSpec((rows, block_width), lambda i, s: (0, 0))] * peers,
            out_specs=pl.BlockSpec((peers * rows, block_width), lambda i, s: (0, 0)),
            scratch_shapes=[pltpu.VMEM((peers * rows, block_width), jnp.bfloat16)],
        ),
        out_shape=jax.ShapeDtypeStruct((peers * rows, block_width), jnp.bfloat16),
        compiler_params=pltpu.CompilerParams(vmem_limit_bytes=VMEM_LIMIT),
        name="gather_tiles",
    )(order, *received)


def project_kernel(swapped, a_ref, w_ref, send_ref, keep_ref):
    acc = jnp.dot(a_ref[...], w_ref[...], preferred_element_type=jnp.float32).astype(jnp.bfloat16)
    quarter = acc.shape[0] // 4
    parts = [acc[i * quarter:(i + 1) * quarter] for i in range(4)]
    if swapped:
        parts = [parts[0], parts[2], parts[1], parts[3]]
    for i in range(2):
        send_ref[pl.ds(i * quarter, quarter), :] = parts[i]
        keep_ref[pl.ds(i * quarter, quarter), :] = parts[2 + i]


def project(a, weight, first, columns, swapped, block=256):
    rows, depth = a.shape
    half = jax.ShapeDtypeStruct((rows // 2, columns), jnp.bfloat16)
    return pl.pallas_call(
        functools.partial(project_kernel, swapped),
        grid=(columns // block,),
        in_specs=[
            pl.BlockSpec((rows, depth), lambda i: (0, 0)),
            pl.BlockSpec((depth, block), lambda i: (0, first // block + i)),
        ],
        out_specs=[pl.BlockSpec((rows // 2, block), lambda i: (0, i))] * 2,
        out_shape=[half, half],
        compiler_params=pltpu.CompilerParams(vmem_limit_bytes=VMEM_LIMIT),
        cost_estimate=pl.CostEstimate(
            flops=2 * rows * depth * columns,
            bytes_accessed=2 * (rows * depth + depth * columns + rows * columns),
            transcendentals=0,
        ),
        name="project",
    )(a, weight)


def finish_kernel(tiles, chunks, columns, scalars, live_ref, bias_ref, *refs):
    out = refs[-1]
    core = scalars[1]
    for index, (half, first) in enumerate(chunks):
        keep, recv = refs[2 * index], refs[2 * index + 1]
        summed = keep[...].astype(jnp.float32) + recv[...].astype(jnp.float32)
        summed += bias_ref[:, first:first + columns]
        act = 0.5 * summed * (1.0 + lax.erf(summed * 0.7071067811865476))
        side = core if half == 0 else 1 - core
        for tile in range(tiles):
            value = jnp.where(live_ref[tile] > 0, act[tile * HALF:(tile + 1) * HALF], 0.0)
            out[tile, side, :, first:first + columns] = value.astype(jnp.bfloat16)


def finish(scalars, live, bias, sums, chunks, columns, tiles):
    width = bias.shape[0]
    flat = [array for pair in sums for array in pair]
    out = pl.pallas_call(
        functools.partial(finish_kernel, tiles, chunks, columns),
        grid_spec=pltpu.PrefetchScalarGridSpec(
            num_scalar_prefetch=2,
            grid=(1,),
            in_specs=[pl.BlockSpec((1, width), lambda i, s, l: (0, 0))]
            + [pl.BlockSpec(array.shape, lambda i, s, l: (0, 0)) for array in flat],
            out_specs=pl.BlockSpec((tiles, 2, HALF, width), lambda i, s, l: (0, 0, 0, 0)),
        ),
        out_shape=jax.ShapeDtypeStruct((tiles, 2, HALF, width), jnp.bfloat16),
        compiler_params=pltpu.CompilerParams(vmem_limit_bytes=VMEM_LIMIT),
        name="finish",
    )(scalars, live, bias.reshape(1, width), *flat)
    return out.reshape(tiles * TILE_ROWS, width)


def exchange(array, mask, peers):
    return lax.ppermute(array, "dp", [(d, d ^ mask) for d in range(peers)])


def halve(send, keep, bits, peers):
    for bit in bits[:-1]:
        recv = exchange(send, 1 << bit, peers)
        half = keep.shape[0] // 2
        summed = keep.astype(jnp.float32) + recv.astype(jnp.float32)
        send, keep = summed[:half].astype(jnp.bfloat16), summed[half:]
    return keep, exchange(send, 1 << bits[-1], peers)


def body(patch_feats, ln_gain, ln_shift, merge_weight, merge_bias, tile_count, tile_dest):
    peers = lax.axis_size("dp")
    me = lax.axis_index("dp").astype(jnp.int32)
    core = lax.axis_index("tensor").astype(jnp.int32)
    tiles = patch_feats.shape[0] // TILE
    slots = peers * tiles
    bits = list(range(peers.bit_length() - 1))
    columns = merge_weight.shape[1]

    source_ids = jnp.arange(peers, dtype=jnp.int32)
    my_count = jnp.sum(jnp.where(source_ids == me, tile_count, 0))
    scalars = jnp.stack([me, core, my_count])
    pieces = prepare(scalars, patch_feats, ln_gain, ln_shift, peers, tiles)

    owners = jnp.array(arrangement(bits), jnp.int32) ^ me
    wanted = (owners[:, None] * tiles + jnp.arange(tiles, dtype=jnp.int32)[None, :]).reshape(slots)
    tile_ids = jnp.arange(slots, dtype=jnp.int32)
    anchor = jnp.sum(jnp.where(tile_dest[None, :] == wanted[:, None], tile_ids[None, :], 0), axis=1)
    source, place = anchor // tiles, anchor % tiles
    order = (source ^ me) * tiles + place
    own_source, own_place = source[-tiles:], place[-tiles:]
    own_count = jnp.sum(jnp.where(own_source[:, None] == source_ids[None, :], tile_count[None, :], 0), axis=1)
    live = (own_place < own_count).astype(jnp.int32)

    received = {0: pieces[0]}
    for k in reversed(range(1, peers)):
        received[k] = exchange(pieces[k], k, peers)
    mine = gather_tiles(order, [received[k] for k in range(peers)])
    other = lax.ppermute(mine, "tensor", [(0, 1), (1, 0)])

    y_first = bits
    z_first = [bits[1], bits[0]] + bits[2:]
    half = columns // 2
    plan = [(0, 0, False), (0, half, True), (1, 0, False), (1, half, False)]
    sums, chunks = [], []
    for side, first, swapped in plan:
        send, keep = project(mine if side == 0 else other, merge_weight, first, half, swapped)
        sums.append(halve(send, keep, z_first if swapped else y_first, peers))
        chunks.append((side, first))
    return finish(scalars, live, merge_bias, sums, chunks, half, tiles)


def solution(mesh):
    in_specs = (
        P(("group", "dp"), None),
        P(),
        P(),
        P("dp", "tensor"),
        P("tensor"),
        P("group"),
        P("group"),
    )
    out_specs = P(("group", "dp"), "tensor")
    return jax.shard_map(body, mesh=mesh, in_specs=in_specs, out_specs=out_specs, check_vma=False)
```

```python
import functools
import math

import jax
import jax.numpy as jnp
from jax import lax
from jax.experimental import pallas as pl
from jax.experimental.pallas import tpu as pltpu
from jax.sharding import PartitionSpec as P

TILE = 128
TILE_ROWS = TILE // 4
PHASES = 2
PART = TILE_ROWS // PHASES
VMEM_LIMIT = 16 * 1024 * 1024
BIG_VMEM = 20 * 1024 * 1024
PROJECT_VMEM = 20 * 1024 * 1024
LANES = 128
STEPS = [(0, 0), (1, 0), (2, -1), (0, 1), (2, 0), (1, 1), (3, 0), (0, 2), (2, 1), (1, 2), (3, 1), (2, 2), (3, 2)]


def arrangement(bits):
    if not bits:
        return [0]
    rest = arrangement(bits[1:])
    return [owner ^ (1 << bits[0]) for owner in rest] + rest


def in_hbm(array):
    return pltpu.with_memory_space_constraint(array, pltpu.HBM)


def routes(peers):
    if peers == 8:
        return [[2, 4, 5, 1], [3, 6, 7, 0]]
    order = list(reversed(range(peers)))
    return [order[0::2], order[1::2]]


def prepare_kernel(peers, tiles, phase, x_hbm, gain_hbm, shift_hbm, count_hbm, *refs):
    outs, (pieces, x_ref, gain_ref, shift_ref, count_ref, sems) = refs[-6 - peers // 2:-6], refs[-6:]
    me, core = lax.axis_index("dp"), lax.axis_index("tensor")
    width = x_hbm.shape[-1]
    total = 4 * width
    block_width = total // peers
    per_patch = width // block_width
    rows = tiles * PART
    copies = [
        pltpu.make_async_copy(x_hbm.at[:, phase], x_ref, sems.at[0]),
        pltpu.make_async_copy(gain_hbm, gain_ref, sems.at[1]),
        pltpu.make_async_copy(shift_hbm, shift_ref, sems.at[2]),
        pltpu.make_async_copy(count_hbm, count_ref, sems.at[3]),
    ]
    for copy in copies:
        copy.start()
    row_out = lax.broadcasted_iota(jnp.int32, (4 * rows, 4 * rows), 0)
    row_in = lax.broadcasted_iota(jnp.int32, (4 * rows, 4 * rows), 1)
    quarter = sum((row_out >= q * rows).astype(jnp.int32) for q in range(1, 4))
    source = 4 * (row_out - quarter * rows) + quarter
    mix = (row_in == source).astype(jnp.bfloat16)
    tile_of = lax.broadcasted_iota(jnp.int32, (rows, 1), 0) // PART
    for copy in copies:
        copy.wait()
    live = tile_of < count_ref[me]
    x = x_ref[...].reshape(4 * rows, width)
    y = jnp.dot(mix, x, preferred_element_type=jnp.float32)
    parts = [y[q * rows:(q + 1) * rows] for q in range(4)]
    mean = sum(jnp.sum(part, axis=1, keepdims=True) for part in parts) / total
    parts = [part - mean for part in parts]
    variance = sum(jnp.sum(part * part, axis=1, keepdims=True) for part in parts) / total
    scale = lax.rsqrt(variance + 1e-06)
    for q in range(4):
        normed = []
        for lane in range(width // LANES):
            at = pl.ds(q * (width // LANES) + lane, 1)
            part = parts[q][:, lane * LANES:(lane + 1) * LANES]
            normed.append(part * scale * gain_ref[at, :] + shift_ref[at, :])
        normed = jnp.concatenate(normed, axis=1)
        normed = jnp.where(live, normed, 0.0).astype(jnp.bfloat16)
        for part in range(per_patch):
            pieces[q * per_patch + part] = normed[:, part * block_width:(part + 1) * block_width]
    for out, first, second in zip(outs, *routes(peers)):
        out[...] = pieces[jnp.bitwise_xor(me, jnp.where(core == 0, first, second))]


def prepare(tile_count, patch_feats, ln_gain, ln_shift, peers, tiles, phase, after):
    width = patch_feats.shape[1]
    block_width = 4 * width // peers
    rows = tiles * PART
    x = patch_feats.reshape(tiles, PHASES, 4 * PART, width)
    vectors = (4 * width // LANES, LANES)
    operands = [x, ln_gain.reshape(vectors), ln_shift.reshape(vectors), tile_count]
    return pl.pallas_call(
        functools.partial(prepare_kernel, peers, tiles, phase),
        in_specs=[pl.BlockSpec(memory_space=pl.ANY)] * (4 + len(after)),
        out_specs=[pl.BlockSpec(memory_space=pltpu.VMEM)] * (peers // 2),
        scratch_shapes=[
            pltpu.VMEM((peers, rows, block_width), jnp.bfloat16),
            pltpu.VMEM((tiles, 4 * PART, width), jnp.bfloat16),
            pltpu.VMEM(vectors, jnp.float32),
            pltpu.VMEM(vectors, jnp.float32),
            pltpu.SMEM(tile_count.shape, jnp.int32),
            pltpu.SemaphoreType.DMA((4,)),
        ],
        out_shape=[pltpu.VMEM((rows, block_width), jnp.bfloat16)] * (peers // 2),
        compiler_params=pltpu.CompilerParams(vmem_limit_bytes=BIG_VMEM),
        cost_estimate=pl.CostEstimate(flops=0, bytes_accessed=32 * rows * width, transcendentals=0),
        name="prepare",
    )(*[in_hbm(operand) for operand in operands], *after)


def scatter_pieces(pieces, peers):
    received = []
    for piece, first, second in zip(pieces, *routes(peers)):
        pairs = [(2 * d, 2 * (d ^ first)) for d in range(peers)]
        pairs += [(2 * d + 1, 2 * (d ^ second) + 1) for d in range(peers) if second != 0]
        received.append(lax.ppermute(piece, ("dp", "tensor"), pairs))
    return received


def pack_kernel(count, own_index, *refs):
    pieces, own, out = refs[:count], refs[count], refs[-1]
    rows, width = own.shape
    if out.shape[1] > width:
        out[:, width:] = jnp.zeros((out.shape[0], out.shape[1] - width), out.dtype)
    for i, piece in enumerate(pieces):
        value = piece[...]
        if i == own_index:
            value = jnp.where(lax.axis_index("tensor") == 0, value, own[...])
        out[i * rows:(i + 1) * rows, :width] = value


def pack(received, own, after):
    own_index = routes(2 * len(received))[1].index(0)
    rows, width = own.shape
    padded = -(-width // LANES) * LANES
    inside = pl.BlockSpec(memory_space=pltpu.VMEM)
    return pl.pallas_call(
        functools.partial(pack_kernel, len(received), own_index),
        in_specs=[inside] * (len(received) + 1) + [pl.BlockSpec(memory_space=pl.ANY)] * len(after),
        out_specs=inside,
        out_shape=pltpu.VMEM((len(received) * rows, padded), jnp.bfloat16),
        compiler_params=pltpu.CompilerParams(vmem_limit_bytes=VMEM_LIMIT),
        name="pack",
    )(*received, own, *after)


def load_kernel(w_hbm, *refs):
    w_ref, sem = refs[-2:]
    copy = pltpu.make_async_copy(w_hbm, w_ref, sem)
    copy.start()
    copy.wait()


def load(array, after):
    return pl.pallas_call(
        load_kernel,
        in_specs=[pl.BlockSpec(memory_space=pl.ANY)] * (1 + len(after)),
        out_specs=pl.BlockSpec(memory_space=pltpu.VMEM),
        out_shape=pltpu.VMEM(array.shape, array.dtype),
        scratch_shapes=[pltpu.SemaphoreType.DMA],
        compiler_params=pltpu.CompilerParams(vmem_limit_bytes=VMEM_LIMIT),
        cost_estimate=pl.CostEstimate(flops=0, bytes_accessed=4 * array.size, transcendentals=0),
        name="load",
    )(in_hbm(array), *after)


def multiply(first, block, a_ref, w_ref, send_ref, keep_ref):
    half = a_ref.shape[0] // 2
    for column in range(0, send_ref.shape[1], block):
        w = w_ref[:, first + column:first + column + block]
        acc = jnp.dot(a_ref[:, :w.shape[0]], w, preferred_element_type=jnp.float32)
        acc = acc.astype(jnp.bfloat16)
        send_ref[:, column:column + block] = acc[:half]
        keep_ref[:, column:column + block] = acc[half:]


def project_kernel(first, block, a_ref, w_ref, *refs):
    multiply(first, block, a_ref, w_ref, *refs[-2:])


def gather_kernel(first, block, order_ref, mine_ref, other_ref, w_ref, *refs):
    sorted_ref, send_ref, keep_ref, held = refs[-4:]
    core = lax.axis_index("tensor")
    held[core] = mine_ref[...]
    held[1 - core] = other_ref[...]
    half = mine_ref.shape[0] // PART
    for i in range(sorted_ref.shape[0] // PART):
        place = order_ref[i]
        side = (place >= half).astype(jnp.int32)
        start = pl.multiple_of((place - side * half) * PART, PART)
        sorted_ref[pl.ds(i * PART, PART), :] = held[side, pl.ds(start, PART), :]
    multiply(first, block, sorted_ref, w_ref, send_ref, keep_ref)


def cost(rows, depth, columns):
    return pl.CostEstimate(
        flops=2 * rows * depth * columns,
        bytes_accessed=2 * (rows * depth + depth * columns + rows * columns),
        transcendentals=0,
    )


def project(a, weight, first, columns, after, block=256):
    rows = a.shape[0]
    depth = weight.shape[0]
    half = pltpu.VMEM((rows // 2, columns), jnp.bfloat16)
    inside, outside = pl.BlockSpec(memory_space=pltpu.VMEM), pl.BlockSpec(memory_space=pl.ANY)
    return pl.pallas_call(
        functools.partial(project_kernel, first, block),
        in_specs=[inside] * 2 + [outside] * len(after),
        out_specs=[inside] * 2,
        out_shape=[half, half],
        compiler_params=pltpu.CompilerParams(vmem_limit_bytes=PROJECT_VMEM),
        cost_estimate=cost(rows, depth, columns),
        name="project",
    )(a, weight, *after)


def gather_and_project(order, mine, other, weight, first, columns, after, block=256):
    rows, padded = mine.shape
    depth = weight.shape[0]
    half = pltpu.VMEM((rows, columns), jnp.bfloat16)
    inside, outside = pl.BlockSpec(memory_space=pltpu.VMEM), pl.BlockSpec(memory_space=pl.ANY)
    return pl.pallas_call(
        functools.partial(gather_kernel, first, block),
        in_specs=[pl.BlockSpec(memory_space=pltpu.SMEM)] + [inside] * 3 + [outside] * len(after),
        out_specs=[inside] * 3,
        out_shape=[pltpu.VMEM((2 * rows, padded), jnp.bfloat16), half, half],
        scratch_shapes=[pltpu.VMEM((2, rows, padded), jnp.bfloat16)],
        compiler_params=pltpu.CompilerParams(vmem_limit_bytes=PROJECT_VMEM),
        cost_estimate=cost(2 * rows, depth, columns),
        name="gather_and_project",
    )(order, mine, other, weight, *after)


def activate(bias_ref, first, keep_ref, recv_ref):
    summed = keep_ref[...].astype(jnp.float32) + recv_ref[...].astype(jnp.float32)
    summed += bias_ref[:, first:first + summed.shape[1]]
    return (0.5 * summed * (1.0 + lax.erf(summed * 0.7071067811865476))).astype(jnp.bfloat16)


def early_kernel(first, bias_ref, keep_ref, recv_ref, *refs):
    refs[-1][...] = activate(bias_ref, first, keep_ref, recv_ref)


def early(bias, first, keep, recv, after):
    inside, outside = pl.BlockSpec(memory_space=pltpu.VMEM), pl.BlockSpec(memory_space=pl.ANY)
    return pl.pallas_call(
        functools.partial(early_kernel, first),
        in_specs=[inside] * 3 + [outside] * len(after),
        out_specs=inside,
        out_shape=pltpu.VMEM(keep.shape, jnp.bfloat16),
        compiler_params=pltpu.CompilerParams(vmem_limit_bytes=VMEM_LIMIT),
        name="early",
    )(bias.reshape(1, -1), keep, recv, *after)


def finish_kernel(tiles, chunks, live_ref, bias_ref, *refs):
    out, refs = refs[-1], list(refs[:-1])
    for phase, first, columns, count in chunks:
        parts, refs = refs[:count], refs[count:]
        value = parts[0][...] if count == 1 else activate(bias_ref, first, *parts)
        for tile in range(tiles):
            rows = value[tile * PART:(tile + 1) * PART]
            rows = jnp.where(live_ref[tile] > 0, rows, jnp.zeros_like(rows))
            out[tile, phase, :, first:first + columns] = rows


def finish(live, bias, chunks, flows, tiles):
    width = bias.shape[0]
    chunks = [chunk + (len(flow),) for chunk, flow in zip(chunks, flows)]
    flat = [array for flow in flows for array in flow]
    inside = pl.BlockSpec(memory_space=pltpu.VMEM)
    out = pl.pallas_call(
        functools.partial(finish_kernel, tiles, chunks),
        in_specs=[pl.BlockSpec(memory_space=pltpu.SMEM), inside] + [inside] * len(flat),
        out_specs=inside,
        out_shape=jax.ShapeDtypeStruct((tiles, PHASES, PART, width), jnp.bfloat16),
        compiler_params=pltpu.CompilerParams(vmem_limit_bytes=VMEM_LIMIT),
        name="finish",
    )(live, bias.reshape(1, width), *flat)
    return out.reshape(tiles * TILE_ROWS, width)


def exchange(array, masks, peers):
    pairs = [(2 * d + core, 2 * (d ^ mask) + core) for core, mask in enumerate(masks) for d in range(peers)]
    return lax.ppermute(array, ("dp", "tensor"), pairs)


def accumulate_kernel(count, *refs):
    send_out, keep_out = refs[-2:]
    half = send_out.shape[0]
    start = 0
    for index in range(count):
        keep_ref, recv_ref = refs[2 * index], refs[2 * index + 1]
        at = slice(start, start + keep_ref.shape[1])
        start = at.stop
        summed = keep_ref[...].astype(jnp.float32) + recv_ref[...].astype(jnp.float32)
        send_out[:, at] = summed[:half].astype(jnp.bfloat16)
        keep_out[:, at] = summed[half:]


def accumulate(flows, after):
    rows = flows[0][0].shape[0] // 2
    columns = sum(keep.shape[1] for keep, _ in flows)
    inside, outside = pl.BlockSpec(memory_space=pltpu.VMEM), pl.BlockSpec(memory_space=pl.ANY)
    return pl.pallas_call(
        functools.partial(accumulate_kernel, len(flows)),
        in_specs=[inside] * (2 * len(flows)) + [outside] * len(after),
        out_specs=[inside, inside],
        out_shape=[pltpu.VMEM((rows, columns), jnp.bfloat16), pltpu.VMEM((rows, columns), jnp.float32)],
        compiler_params=pltpu.CompilerParams(vmem_limit_bytes=VMEM_LIMIT),
        name="accumulate",
    )(*[array for flow in flows for array in flow], *after)


def body(patch_feats, ln_gain, ln_shift, merge_weight, merge_bias, tile_count, tile_dest):
    peers = lax.axis_size("dp")
    me = lax.axis_index("dp").astype(jnp.int32)
    tiles = patch_feats.shape[0] // TILE
    slots = peers * tiles
    bits = list(range(peers.bit_length() - 1))
    columns = merge_weight.shape[1]

    source_ids = jnp.arange(peers, dtype=jnp.int32)
    sequences = [bits, [bits[1], bits[0]] + bits[2:]]
    first_core = (lax.axis_index("tensor") == 0).astype(jnp.int32)
    owners = [jnp.array(arrangement(sequence), jnp.int32) for sequence in sequences]
    owners = jnp.where(first_core == 1, *owners) ^ me
    wanted = (owners[:, None] * tiles + jnp.arange(tiles, dtype=jnp.int32)[None, :]).reshape(slots)
    tile_ids = jnp.arange(slots, dtype=jnp.int32)
    anchor = jnp.sum(jnp.where(tile_dest[None, :] == wanted[:, None], tile_ids[None, :], 0), axis=1)
    source, place = anchor // tiles, anchor % tiles
    sequence = jnp.array(sum(routes(peers), []), jnp.int32)
    is_there = sequence[None, :] == (source ^ me)[:, None]
    order = jnp.sum(jnp.where(is_there, source_ids[None, :], 0), axis=1) * tiles + place
    own_source, own_place = source[-tiles:], place[-tiles:]
    own_count = jnp.sum(jnp.where(own_source[:, None] == source_ids[None, :], tile_count[None, :], 0), axis=1)
    live = (own_place < own_count).astype(jnp.int32)

    half = columns // 2
    chunks = [(0, 0, half), (0, half, half), (1, 0, half), (1, half, half)]
    pieces = [prepare(tile_count, patch_feats, ln_gain, ln_shift, peers, tiles, 0, [])]
    pieces.append(prepare(tile_count, patch_feats, ln_gain, ln_shift, peers, tiles, 1, pieces[0][:1]))
    scattered = [scatter_pieces(parts, peers) for parts in pieces]
    packed = {}

    flows, done, after = {}, {}, []
    steps = STEPS
    if len(bits) != 3:
        steps = [(index, step) for step in range(len(bits)) for index in range(len(chunks))]
    for index, step in steps:
        phase, first, count = chunks[index]
        if step < 0 or (step == 0 and first == 0 and phase not in packed):
            mine = pack(scattered[phase], pieces[phase][routes(peers)[1].index(0)], after)
            packed[phase] = mine, lax.ppermute(mine, "tensor", [(0, 1), (1, 0)])
            after = [mine]
            if phase == 0:
                weight = load(merge_weight, after)
            if step < 0:
                continue
        if step == len(bits):
            done[index] = early(merge_bias, first, *flows[index], after)
            after = [done[index]]
            continue
        if step > 0:
            send, keep = accumulate([flows[index]], after)
        elif first == 0:
            rows, send, keep = gather_and_project(order, *packed[phase], weight, first, count, after)
        else:
            send, keep = project(rows, weight, first, count, after)
        after = [keep]
        flows[index] = (keep, exchange(send, [1 << sequence[step] for sequence in sequences], peers))
    flows = [(done[i],) if i in done else flows[i] for i in range(len(chunks))]
    return finish(live, merge_bias, chunks, flows, tiles)


def solution(mesh):
    in_specs = (
        P(("group", "dp"), None),
        P(),
        P(),
        P("dp", "tensor"),
        P("tensor"),
        P("group"),
        P("group"),
    )
    out_specs = P(("group", "dp"), "tensor")
    return jax.shard_map(body, mesh=mesh, in_specs=in_specs, out_specs=out_specs, check_vma=False)
```

```python
import functools
import math

import jax
import jax.numpy as jnp
from jax import lax
from jax.experimental import pallas as pl
from jax.experimental.pallas import tpu as pltpu
from jax.sharding import PartitionSpec as P

TILE = 128
TILE_ROWS = TILE // 4
PHASES = 2
PART = TILE_ROWS // PHASES
VMEM_LIMIT = 16 * 1024 * 1024
BIG_VMEM = 20 * 1024 * 1024
PROJECT_VMEM = 20 * 1024 * 1024
LANES = 128
STEPS = [(0, 0), (1, -1), (1, 0), (0, 1), (2, 0), (1, 1), (2, 1), (0, 2), (1, 2), (0, 3), (2, 2)]


def arrangement(bits):
    if not bits:
        return [0]
    rest = arrangement(bits[1:])
    return [owner ^ (1 << bits[0]) for owner in rest] + rest


def in_hbm(array):
    return pltpu.with_memory_space_constraint(array, pltpu.HBM)


def routes(peers):
    if peers == 8:
        return [[2, 4, 5, 1], [3, 6, 7, 0]]
    order = list(reversed(range(peers)))
    return [order[0::2], order[1::2]]


def prepare_kernel(peers, tiles, phase, x_hbm, gain_hbm, shift_hbm, count_hbm, *refs):
    outs, (pieces, x_ref, gain_ref, shift_ref, count_ref, sems) = refs[-6 - peers // 2:-6], refs[-6:]
    if phase == 1:
        outs[-1][:tiles * PART, :] = refs[0][...]
    me, core = lax.axis_index("dp"), lax.axis_index("tensor")
    width = x_hbm.shape[-1]
    total = 4 * width
    block_width = total // peers
    per_patch = width // block_width
    rows = tiles * PART
    copies = [
        pltpu.make_async_copy(x_hbm.at[:, phase], x_ref, sems.at[0]),
        pltpu.make_async_copy(gain_hbm, gain_ref, sems.at[1]),
        pltpu.make_async_copy(shift_hbm, shift_ref, sems.at[2]),
        pltpu.make_async_copy(count_hbm, count_ref, sems.at[3]),
    ]
    for copy in copies:
        copy.start()
    row_out = lax.broadcasted_iota(jnp.int32, (4 * rows, 4 * rows), 0)
    row_in = lax.broadcasted_iota(jnp.int32, (4 * rows, 4 * rows), 1)
    quarter = sum((row_out >= q * rows).astype(jnp.int32) for q in range(1, 4))
    source = 4 * (row_out - quarter * rows) + quarter
    mix = (row_in == source).astype(jnp.bfloat16)
    tile_of = lax.broadcasted_iota(jnp.int32, (rows, 1), 0) // PART
    for copy in copies:
        copy.wait()
    live = tile_of < count_ref[me]
    x = x_ref[...].reshape(4 * rows, width)
    y = jnp.dot(mix, x, preferred_element_type=jnp.float32)
    parts = [y[q * rows:(q + 1) * rows] for q in range(4)]
    mean = sum(jnp.sum(part, axis=1, keepdims=True) for part in parts) / total
    parts = [part - mean for part in parts]
    variance = sum(jnp.sum(part * part, axis=1, keepdims=True) for part in parts) / total
    scale = lax.rsqrt(variance + 1e-06)
    for q in range(4):
        normed = []
        for lane in range(width // LANES):
            at = pl.ds(q * (width // LANES) + lane, 1)
            part = parts[q][:, lane * LANES:(lane + 1) * LANES]
            normed.append(part * scale * gain_ref[at, :] + shift_ref[at, :])
        normed = jnp.concatenate(normed, axis=1)
        normed = jnp.where(live, normed, 0.0).astype(jnp.bfloat16)
        for part in range(per_patch):
            pieces[q * per_patch + part] = normed[:, part * block_width:(part + 1) * block_width]
    for out, first, second in zip(outs, *routes(peers)):
        value = pieces[jnp.bitwise_xor(me, jnp.where(core == 0, first, second))]
        out[out.shape[0] - tiles * PART:, :] = value


def prepare(tile_count, patch_feats, ln_gain, ln_shift, peers, tiles, phase, last, after):
    width = patch_feats.shape[1]
    block_width = 4 * width // peers
    rows = tiles * PART
    x = patch_feats.reshape(tiles, PHASES, 4 * PART, width)
    vectors = (4 * width // LANES, LANES)
    inside = pl.BlockSpec(memory_space=pltpu.VMEM)
    operands = [x, ln_gain.reshape(vectors), ln_shift.reshape(vectors), tile_count]
    return pl.pallas_call(
        functools.partial(prepare_kernel, peers, tiles, phase),
        in_specs=[pl.BlockSpec(memory_space=pl.ANY)] * 4 + [inside] * len(last) + [pl.BlockSpec(memory_space=pl.ANY)] * len(after),
        out_specs=[inside] * (peers // 2),
        scratch_shapes=[
            pltpu.VMEM((peers, rows, block_width), jnp.bfloat16),
            pltpu.VMEM((tiles, 4 * PART, width), jnp.bfloat16),
            pltpu.VMEM(vectors, jnp.float32),
            pltpu.VMEM(vectors, jnp.float32),
            pltpu.SMEM(tile_count.shape, jnp.int32),
            pltpu.SemaphoreType.DMA((4,)),
        ],
        out_shape=[pltpu.VMEM((rows, block_width), jnp.bfloat16)] * (peers // 2 - 1)
        + [pltpu.VMEM(((1 + len(last)) * rows, block_width), jnp.bfloat16)],
        compiler_params=pltpu.CompilerParams(vmem_limit_bytes=BIG_VMEM),
        cost_estimate=pl.CostEstimate(flops=0, bytes_accessed=32 * rows * width, transcendentals=0),
        name="prepare",
    )(*[in_hbm(operand) for operand in operands], *last, *after)


def send_piece(piece, index, peers):
    first, second = (route[index] for route in routes(peers))
    pairs = [(2 * d, 2 * (d ^ first)) for d in range(peers)]
    pairs += [(2 * d + 1, 2 * (d ^ second) + 1) for d in range(peers) if second != 0]
    return lax.ppermute(piece, ("dp", "tensor"), pairs)


def pack_kernel(count, phase, *refs):
    pieces, last, own, out = refs[:count], refs[count], refs[count + 1], refs[-1]
    rows, width = pieces[0].shape
    if out.shape[1] > width:
        out[:, width:] = jnp.zeros((out.shape[0], out.shape[1] - width), out.dtype)
    for i, piece in enumerate(pieces):
        out[i * rows:(i + 1) * rows, :width] = piece[...]
    at = slice(phase * rows, (phase + 1) * rows)
    out[count * rows:, :width] = jnp.where(lax.axis_index("tensor") == 0, last[at, :], own[at, :])


def pack(received, last, own, phase, after):
    rows, width = received[0].shape
    padded = -(-width // LANES) * LANES
    inside = pl.BlockSpec(memory_space=pltpu.VMEM)
    return pl.pallas_call(
        functools.partial(pack_kernel, len(received), phase),
        in_specs=[inside] * (len(received) + 2) + [pl.BlockSpec(memory_space=pl.ANY)] * len(after),
        out_specs=inside,
        out_shape=pltpu.VMEM(((len(received) + 1) * rows, padded), jnp.bfloat16),
        compiler_params=pltpu.CompilerParams(vmem_limit_bytes=VMEM_LIMIT),
        name="pack",
    )(*received, last, own, *after)


def load_kernel(w_hbm, *refs):
    w_ref, sem = refs[-2:]
    copy = pltpu.make_async_copy(w_hbm, w_ref, sem)
    copy.start()
    copy.wait()


def load(array, after):
    return pl.pallas_call(
        load_kernel,
        in_specs=[pl.BlockSpec(memory_space=pl.ANY)] * (1 + len(after)),
        out_specs=pl.BlockSpec(memory_space=pltpu.VMEM),
        out_shape=pltpu.VMEM(array.shape, array.dtype),
        scratch_shapes=[pltpu.SemaphoreType.DMA],
        compiler_params=pltpu.CompilerParams(vmem_limit_bytes=VMEM_LIMIT),
        cost_estimate=pl.CostEstimate(flops=0, bytes_accessed=4 * array.size, transcendentals=0),
        name="load",
    )(in_hbm(array), *after)


def multiply(first, block, a_ref, w_ref, send_ref, keep_ref):
    half = a_ref.shape[0] // 2
    for column in range(0, send_ref.shape[1], block):
        w = w_ref[:, first + column:first + column + block]
        acc = jnp.dot(a_ref[:, :w.shape[0]], w, preferred_element_type=jnp.float32)
        acc = acc.astype(jnp.bfloat16)
        send_ref[:, column:column + block] = acc[:half]
        keep_ref[:, column:column + block] = acc[half:]


def project_kernel(first, block, a_ref, w_ref, *refs):
    multiply(first, block, a_ref, w_ref, *refs[-2:])


def gather_kernel(first, block, count, order_ref, mine_ref, other_ref, w_ref, *refs):
    sorted_ref, send_ref, keep_ref = refs[-4 - count:-1 - count]
    held = refs[-1]
    for piece, out in zip(refs[:count], refs[-1 - count:-1]):
        out[...] = piece[...]
    core = lax.axis_index("tensor")
    held[core] = mine_ref[...]
    held[1 - core] = other_ref[...]
    half = mine_ref.shape[0] // PART
    for i in range(sorted_ref.shape[0] // PART):
        place = order_ref[i]
        side = (place >= half).astype(jnp.int32)
        start = pl.multiple_of((place - side * half) * PART, PART)
        sorted_ref[pl.ds(i * PART, PART), :] = held[side, pl.ds(start, PART), :]
    multiply(first, block, sorted_ref, w_ref, send_ref, keep_ref)


def cost(rows, depth, columns):
    return pl.CostEstimate(
        flops=2 * rows * depth * columns,
        bytes_accessed=2 * (rows * depth + depth * columns + rows * columns),
        transcendentals=0,
    )


def project(a, weight, first, columns, after, block=256):
    rows = a.shape[0]
    depth = weight.shape[0]
    half = pltpu.VMEM((rows // 2, columns), jnp.bfloat16)
    inside, outside = pl.BlockSpec(memory_space=pltpu.VMEM), pl.BlockSpec(memory_space=pl.ANY)
    return pl.pallas_call(
        functools.partial(project_kernel, first, block),
        in_specs=[inside] * 2 + [outside] * len(after),
        out_specs=[inside] * 2,
        out_shape=[half, half],
        compiler_params=pltpu.CompilerParams(vmem_limit_bytes=PROJECT_VMEM),
        cost_estimate=cost(rows, depth, columns),
        name="project",
    )(a, weight, *after)


def gather_and_project(order, mine, other, weight, first, columns, pieces, after, block=256):
    rows, padded = mine.shape
    depth = weight.shape[0]
    half = pltpu.VMEM((rows, columns), jnp.bfloat16)
    inside, outside = pl.BlockSpec(memory_space=pltpu.VMEM), pl.BlockSpec(memory_space=pl.ANY)
    return pl.pallas_call(
        functools.partial(gather_kernel, first, block, len(pieces)),
        in_specs=[pl.BlockSpec(memory_space=pltpu.SMEM)] + [inside] * (3 + len(pieces)) + [outside] * len(after),
        out_specs=[inside] * (3 + len(pieces)),
        out_shape=[pltpu.VMEM((2 * rows, padded), jnp.bfloat16), half, half]
        + [pltpu.VMEM(piece.shape, piece.dtype) for piece in pieces],
        scratch_shapes=[pltpu.VMEM((2, rows, padded), jnp.bfloat16)],
        compiler_params=pltpu.CompilerParams(vmem_limit_bytes=PROJECT_VMEM),
        cost_estimate=cost(2 * rows, depth, columns),
        name="gather_and_project",
    )(order, mine, other, weight, *pieces, *after)


def activate(bias_ref, first, keep_ref, recv_ref):
    summed = keep_ref[...].astype(jnp.float32) + recv_ref[...].astype(jnp.float32)
    summed += bias_ref[:, first:first + summed.shape[1]]
    return (0.5 * summed * (1.0 + lax.erf(summed * 0.7071067811865476))).astype(jnp.bfloat16)


def early_kernel(first, bias_ref, keep_ref, recv_ref, *refs):
    refs[-1][...] = activate(bias_ref, first, keep_ref, recv_ref)


def early(bias, first, keep, recv, after):
    inside, outside = pl.BlockSpec(memory_space=pltpu.VMEM), pl.BlockSpec(memory_space=pl.ANY)
    return pl.pallas_call(
        functools.partial(early_kernel, first),
        in_specs=[inside] * 3 + [outside] * len(after),
        out_specs=inside,
        out_shape=pltpu.VMEM(keep.shape, jnp.bfloat16),
        compiler_params=pltpu.CompilerParams(vmem_limit_bytes=VMEM_LIMIT),
        name="early",
    )(bias.reshape(1, -1), keep, recv, *after)


def finish_kernel(tiles, chunks, live_ref, bias_ref, *refs):
    out, refs = refs[-1], list(refs[:-1])
    for phase, first, columns, count in chunks:
        parts, refs = refs[:count], refs[count:]
        value = parts[0][...] if count == 1 else activate(bias_ref, first, *parts)
        for tile in range(tiles):
            rows = value[tile * PART:(tile + 1) * PART]
            rows = jnp.where(live_ref[tile] > 0, rows, jnp.zeros_like(rows))
            out[tile, phase, :, first:first + columns] = rows


def finish(live, bias, chunks, flows, tiles):
    width = bias.shape[0]
    chunks = [chunk + (len(flow),) for chunk, flow in zip(chunks, flows)]
    flat = [array for flow in flows for array in flow]
    inside = pl.BlockSpec(memory_space=pltpu.VMEM)
    out = pl.pallas_call(
        functools.partial(finish_kernel, tiles, chunks),
        in_specs=[pl.BlockSpec(memory_space=pltpu.SMEM), inside] + [inside] * len(flat),
        out_specs=inside,
        out_shape=jax.ShapeDtypeStruct((tiles, PHASES, PART, width), jnp.bfloat16),
        compiler_params=pltpu.CompilerParams(vmem_limit_bytes=VMEM_LIMIT),
        name="finish",
    )(live, bias.reshape(1, width), *flat)
    return out.reshape(tiles * TILE_ROWS, width)


def exchange(array, masks, peers):
    pairs = [(2 * d + core, 2 * (d ^ mask) + core) for core, mask in enumerate(masks) for d in range(peers)]
    return lax.ppermute(array, ("dp", "tensor"), pairs)


def accumulate_kernel(count, *refs):
    send_out, keep_out = refs[-2:]
    half = send_out.shape[0]
    start = 0
    for index in range(count):
        keep_ref, recv_ref = refs[2 * index], refs[2 * index + 1]
        at = slice(start, start + keep_ref.shape[1])
        start = at.stop
        summed = keep_ref[...].astype(jnp.float32) + recv_ref[...].astype(jnp.float32)
        send_out[:, at] = summed[:half].astype(jnp.bfloat16)
        keep_out[:, at] = summed[half:]


def accumulate(flows, after):
    rows = flows[0][0].shape[0] // 2
    columns = sum(keep.shape[1] for keep, _ in flows)
    inside, outside = pl.BlockSpec(memory_space=pltpu.VMEM), pl.BlockSpec(memory_space=pl.ANY)
    return pl.pallas_call(
        functools.partial(accumulate_kernel, len(flows)),
        in_specs=[inside] * (2 * len(flows)) + [outside] * len(after),
        out_specs=[inside, inside],
        out_shape=[pltpu.VMEM((rows, columns), jnp.bfloat16), pltpu.VMEM((rows, columns), jnp.float32)],
        compiler_params=pltpu.CompilerParams(vmem_limit_bytes=VMEM_LIMIT),
        name="accumulate",
    )(*[array for flow in flows for array in flow], *after)


def body(patch_feats, ln_gain, ln_shift, merge_weight, merge_bias, tile_count, tile_dest):
    peers = lax.axis_size("dp")
    me = lax.axis_index("dp").astype(jnp.int32)
    tiles = patch_feats.shape[0] // TILE
    slots = peers * tiles
    bits = list(range(peers.bit_length() - 1))
    columns = merge_weight.shape[1]

    source_ids = jnp.arange(peers, dtype=jnp.int32)
    y_first, z_first = bits, [bits[1], bits[0]] + bits[2:]
    is_first = lax.axis_index("tensor") == 0
    tile_ids = jnp.arange(slots, dtype=jnp.int32)
    sent = jnp.array(sum(routes(peers), []), jnp.int32)
    all_sequences, orders = [(y_first, z_first), (y_first, z_first)], []
    for sequences in all_sequences:
        owners = [jnp.array(arrangement(sequence), jnp.int32) for sequence in sequences]
        owners = jnp.where(is_first, *owners) ^ me
        wanted = (owners[:, None] * tiles + jnp.arange(tiles, dtype=jnp.int32)[None, :]).reshape(slots)
        anchor = jnp.sum(jnp.where(tile_dest[None, :] == wanted[:, None], tile_ids[None, :], 0), axis=1)
        source, place = anchor // tiles, anchor % tiles
        is_there = sent[None, :] == (source ^ me)[:, None]
        orders.append(jnp.sum(jnp.where(is_there, source_ids[None, :], 0), axis=1) * tiles + place)
    own_source, own_place = source[-tiles:], place[-tiles:]
    own_count = jnp.sum(jnp.where(own_source[:, None] == source_ids[None, :], tile_count[None, :], 0), axis=1)
    live = (own_place < own_count).astype(jnp.int32)

    half = columns // 2
    chunks = [(0, 0, columns), (1, 0, half), (1, half, half)]
    pieces = [prepare(tile_count, patch_feats, ln_gain, ln_shift, peers, tiles, 0, [], [])]
    pieces.append(prepare(tile_count, patch_feats, ln_gain, ln_shift, peers, tiles, 1, pieces[0][-1:], pieces[0][:1]))
    received = [[send_piece(piece, i, peers) for i, piece in enumerate(parts[:-1])] for parts in pieces]
    last = send_piece(pieces[1][-1], peers // 2 - 1, peers)
    packed = {}

    flows, done, after = {}, {}, []
    steps = STEPS
    if len(bits) != 3:
        steps = [(index, step) for step in range(len(bits)) for index in range(len(chunks))]
    for index, step in steps:
        phase, first, count = chunks[index]
        if step < 0 or (step == 0 and first == 0 and phase not in packed):
            mine = pack(received[phase], last, pieces[1][-1], phase, after)
            packed[phase] = mine, lax.ppermute(mine, "tensor", [(0, 1), (1, 0)])
            after = [mine]
            if phase == 0:
                weight = load(merge_weight, after)
            if step < 0:
                continue
        if step == len(bits):
            done[index] = early(merge_bias, first, *flows[index], after)
            after = [done[index]]
            continue
        if step > 0:
            send, keep = accumulate([flows[index]], after)
        elif first == 0:
            rows, send, keep = gather_and_project(orders[phase], *packed[phase], weight, first, count, [], after)
        else:
            send, keep = project(rows, weight, first, count, after)
        after = [keep]
        flows[index] = (keep, exchange(send, [1 << sequence[step] for sequence in all_sequences[phase]], peers))
    flows = [(done[i],) if i in done else flows[i] for i in range(len(chunks))]
    return finish(live, merge_bias, chunks, flows, tiles)


def solution(mesh):
    in_specs = (
        P(("group", "dp"), None),
        P(),
        P(),
        P("dp", "tensor"),
        P("tensor"),
        P("group"),
        P("group"),
    )
    out_specs = P(("group", "dp"), "tensor")
    return jax.shard_map(body, mesh=mesh, in_specs=in_specs, out_specs=out_specs, check_vma=False)
```

```python
import functools
import math

import jax
import jax.numpy as jnp
from jax import lax
from jax.experimental import pallas as pl
from jax.experimental.pallas import tpu as pltpu
from jax.sharding import PartitionSpec as P

TILE = 128
TILE_ROWS = TILE // 4
PHASES = 2
PART = TILE_ROWS // PHASES
VMEM_LIMIT = 16 * 1024 * 1024
BIG_VMEM = 20 * 1024 * 1024
PROJECT_VMEM = 20 * 1024 * 1024
LANES = 128
STEPS = [(0, 0), (1, -1), (1, 0), (0, 1), (2, 0), (1, 1), (0, 2), (2, 1), (1, 2), (0, 3), (2, 2)]


def arrangement(bits):
    if not bits:
        return [0]
    rest = arrangement(bits[1:])
    return [owner ^ (1 << bits[0]) for owner in rest] + rest


def in_hbm(array):
    return pltpu.with_memory_space_constraint(array, pltpu.HBM)


def routes(peers):
    if peers == 8:
        return [[2, 4, 5, 1], [3, 6, 7, 0]]
    order = list(reversed(range(peers)))
    return [order[0::2], order[1::2]]


def prepare_kernel(peers, tiles, phase, x_hbm, gain_hbm, shift_hbm, count_hbm, *refs):
    outs, (pieces, x_ref, gain_ref, shift_ref, count_ref, sems) = refs[-6 - peers // 2:-6], refs[-6:]
    if phase == 1:
        outs[-1][:tiles * PART, :] = refs[0][...]
    me, core = lax.axis_index("dp"), lax.axis_index("tensor")
    width = x_hbm.shape[-1]
    total = 4 * width
    block_width = total // peers
    per_patch = width // block_width
    rows = tiles * PART
    copies = [
        pltpu.make_async_copy(x_hbm.at[:, phase], x_ref, sems.at[0]),
        pltpu.make_async_copy(gain_hbm, gain_ref, sems.at[1]),
        pltpu.make_async_copy(shift_hbm, shift_ref, sems.at[2]),
        pltpu.make_async_copy(count_hbm, count_ref, sems.at[3]),
    ]
    for copy in copies:
        copy.start()
    row_out = lax.broadcasted_iota(jnp.int32, (4 * rows, 4 * rows), 0)
    row_in = lax.broadcasted_iota(jnp.int32, (4 * rows, 4 * rows), 1)
    quarter = sum((row_out >= q * rows).astype(jnp.int32) for q in range(1, 4))
    source = 4 * (row_out - quarter * rows) + quarter
    mix = (row_in == source).astype(jnp.bfloat16)
    tile_of = lax.broadcasted_iota(jnp.int32, (rows, 1), 0) // PART
    for copy in copies:
        copy.wait()
    live = tile_of < count_ref[me]
    x = x_ref[...].reshape(4 * rows, width)
    y = jnp.dot(mix, x, preferred_element_type=jnp.float32)
    parts = [y[q * rows:(q + 1) * rows] for q in range(4)]
    mean = sum(jnp.sum(part, axis=1, keepdims=True) for part in parts) / total
    parts = [part - mean for part in parts]
    variance = sum(jnp.sum(part * part, axis=1, keepdims=True) for part in parts) / total
    scale = lax.rsqrt(variance + 1e-06)
    for q in range(4):
        normed = []
        for lane in range(width // LANES):
            at = pl.ds(q * (width // LANES) + lane, 1)
            part = parts[q][:, lane * LANES:(lane + 1) * LANES]
            normed.append(part * scale * gain_ref[at, :] + shift_ref[at, :])
        normed = jnp.concatenate(normed, axis=1)
        normed = jnp.where(live, normed, 0.0).astype(jnp.bfloat16)
        for part in range(per_patch):
            pieces[q * per_patch + part] = normed[:, part * block_width:(part + 1) * block_width]
    for out, first, second in zip(outs, *routes(peers)):
        value = pieces[jnp.bitwise_xor(me, jnp.where(core == 0, first, second))]
        out[out.shape[0] - tiles * PART:, :] = value


def prepare(tile_count, patch_feats, ln_gain, ln_shift, peers, tiles, phase, last, after):
    width = patch_feats.shape[1]
    block_width = 4 * width // peers
    rows = tiles * PART
    x = patch_feats.reshape(tiles, PHASES, 4 * PART, width)
    vectors = (4 * width // LANES, LANES)
    inside = pl.BlockSpec(memory_space=pltpu.VMEM)
    operands = [x, ln_gain.reshape(vectors), ln_shift.reshape(vectors), tile_count]
    return pl.pallas_call(
        functools.partial(prepare_kernel, peers, tiles, phase),
        in_specs=[pl.BlockSpec(memory_space=pl.ANY)] * 4 + [inside] * len(last) + [pl.BlockSpec(memory_space=pl.ANY)] * len(after),
        out_specs=[inside] * (peers // 2),
        scratch_shapes=[
            pltpu.VMEM((peers, rows, block_width), jnp.bfloat16),
            pltpu.VMEM((tiles, 4 * PART, width), jnp.bfloat16),
            pltpu.VMEM(vectors, jnp.float32),
            pltpu.VMEM(vectors, jnp.float32),
            pltpu.SMEM(tile_count.shape, jnp.int32),
            pltpu.SemaphoreType.DMA((4,)),
        ],
        out_shape=[pltpu.VMEM((rows, block_width), jnp.bfloat16)] * (peers // 2 - 1)
        + [pltpu.VMEM(((1 + len(last)) * rows, block_width), jnp.bfloat16)],
        compiler_params=pltpu.CompilerParams(vmem_limit_bytes=BIG_VMEM),
        cost_estimate=pl.CostEstimate(flops=0, bytes_accessed=32 * rows * width, transcendentals=0),
        name="prepare",
    )(*[in_hbm(operand) for operand in operands], *last, *after)


def send_piece(piece, index, peers):
    first, second = (route[index] for route in routes(peers))
    pairs = [(2 * d, 2 * (d ^ first)) for d in range(peers)]
    pairs += [(2 * d + 1, 2 * (d ^ second) + 1) for d in range(peers) if second != 0]
    return lax.ppermute(piece, ("dp", "tensor"), pairs)


def pack_kernel(count, phase, *refs):
    pieces, last, own, out = refs[:count], refs[count], refs[count + 1], refs[-1]
    rows, width = pieces[0].shape
    if out.shape[1] > width:
        out[:, width:] = jnp.zeros((out.shape[0], out.shape[1] - width), out.dtype)
    for i, piece in enumerate(pieces):
        out[i * rows:(i + 1) * rows, :width] = piece[...]
    at = slice(phase * rows, (phase + 1) * rows)
    out[count * rows:, :width] = jnp.where(lax.axis_index("tensor") == 0, last[at, :], own[at, :])


def pack(received, last, own, phase, after):
    rows, width = received[0].shape
    padded = -(-width // LANES) * LANES
    inside = pl.BlockSpec(memory_space=pltpu.VMEM)
    return pl.pallas_call(
        functools.partial(pack_kernel, len(received), phase),
        in_specs=[inside] * (len(received) + 2) + [pl.BlockSpec(memory_space=pl.ANY)] * len(after),
        out_specs=inside,
        out_shape=pltpu.VMEM(((len(received) + 1) * rows, padded), jnp.bfloat16),
        compiler_params=pltpu.CompilerParams(vmem_limit_bytes=VMEM_LIMIT),
        name="pack",
    )(*received, last, own, *after)


def load_kernel(w_hbm, *refs):
    w_ref, sem = refs[-2:]
    copy = pltpu.make_async_copy(w_hbm, w_ref, sem)
    copy.start()
    copy.wait()


def load(array, after):
    return pl.pallas_call(
        load_kernel,
        in_specs=[pl.BlockSpec(memory_space=pl.ANY)] * (1 + len(after)),
        out_specs=pl.BlockSpec(memory_space=pltpu.VMEM),
        out_shape=pltpu.VMEM(array.shape, array.dtype),
        scratch_shapes=[pltpu.SemaphoreType.DMA],
        compiler_params=pltpu.CompilerParams(vmem_limit_bytes=VMEM_LIMIT),
        cost_estimate=pl.CostEstimate(flops=0, bytes_accessed=4 * array.size, transcendentals=0),
        name="load",
    )(in_hbm(array), *after)


def multiply(first, block, a_ref, w_ref, send_ref, keep_ref):
    half = a_ref.shape[0] // 2
    for column in range(0, send_ref.shape[1], block):
        w = w_ref[:, first + column:first + column + block]
        acc = jnp.dot(a_ref[:, :w.shape[0]], w, preferred_element_type=jnp.float32)
        acc = acc.astype(jnp.bfloat16)
        send_ref[:, column:column + block] = acc[:half]
        keep_ref[:, column:column + block] = acc[half:]


def project_kernel(first, block, a_ref, w_ref, *refs):
    multiply(first, block, a_ref, w_ref, *refs[-2:])


def gather_kernel(first, block, count, order_ref, mine_ref, other_ref, w_ref, *refs):
    sorted_ref, send_ref, keep_ref = refs[-4 - count:-1 - count]
    held = refs[-1]
    for piece, out in zip(refs[:count], refs[-1 - count:-1]):
        out[...] = piece[...]
    core = lax.axis_index("tensor")
    held[core] = mine_ref[...]
    held[1 - core] = other_ref[...]
    half = mine_ref.shape[0] // PART
    for i in range(sorted_ref.shape[0] // PART):
        place = order_ref[i]
        side = (place >= half).astype(jnp.int32)
        start = pl.multiple_of((place - side * half) * PART, PART)
        sorted_ref[pl.ds(i * PART, PART), :] = held[side, pl.ds(start, PART), :]
    multiply(first, block, sorted_ref, w_ref, send_ref, keep_ref)


def cost(rows, depth, columns):
    return pl.CostEstimate(
        flops=2 * rows * depth * columns,
        bytes_accessed=2 * (rows * depth + depth * columns + rows * columns),
        transcendentals=0,
    )


def project(a, weight, first, columns, after, block=256):
    rows = a.shape[0]
    depth = weight.shape[0]
    half = pltpu.VMEM((rows // 2, columns), jnp.bfloat16)
    inside, outside = pl.BlockSpec(memory_space=pltpu.VMEM), pl.BlockSpec(memory_space=pl.ANY)
    return pl.pallas_call(
        functools.partial(project_kernel, first, block),
        in_specs=[inside] * 2 + [outside] * len(after),
        out_specs=[inside] * 2,
        out_shape=[half, half],
        compiler_params=pltpu.CompilerParams(vmem_limit_bytes=PROJECT_VMEM),
        cost_estimate=cost(rows, depth, columns),
        name="project",
    )(a, weight, *after)


def gather_and_project(order, mine, other, weight, first, columns, pieces, after, block=256):
    rows, padded = mine.shape
    depth = weight.shape[0]
    half = pltpu.VMEM((rows, columns), jnp.bfloat16)
    inside, outside = pl.BlockSpec(memory_space=pltpu.VMEM), pl.BlockSpec(memory_space=pl.ANY)
    return pl.pallas_call(
        functools.partial(gather_kernel, first, block, len(pieces)),
        in_specs=[pl.BlockSpec(memory_space=pltpu.SMEM)] + [inside] * (3 + len(pieces)) + [outside] * len(after),
        out_specs=[inside] * (3 + len(pieces)),
        out_shape=[pltpu.VMEM((2 * rows, padded), jnp.bfloat16), half, half]
        + [pltpu.VMEM(piece.shape, piece.dtype) for piece in pieces],
        scratch_shapes=[pltpu.VMEM((2, rows, padded), jnp.bfloat16)],
        compiler_params=pltpu.CompilerParams(vmem_limit_bytes=PROJECT_VMEM),
        cost_estimate=cost(2 * rows, depth, columns),
        name="gather_and_project",
    )(order, mine, other, weight, *pieces, *after)


def activate(bias_ref, first, keep_ref, recv_ref):
    summed = keep_ref[...].astype(jnp.float32) + recv_ref[...].astype(jnp.float32)
    summed += bias_ref[:, first:first + summed.shape[1]]
    return (0.5 * summed * (1.0 + lax.erf(summed * 0.7071067811865476))).astype(jnp.bfloat16)


def early_kernel(first, bias_ref, keep_ref, recv_ref, *refs):
    refs[-1][...] = activate(bias_ref, first, keep_ref, recv_ref)


def early(bias, first, keep, recv, after):
    inside, outside = pl.BlockSpec(memory_space=pltpu.VMEM), pl.BlockSpec(memory_space=pl.ANY)
    return pl.pallas_call(
        functools.partial(early_kernel, first),
        in_specs=[inside] * 3 + [outside] * len(after),
        out_specs=inside,
        out_shape=pltpu.VMEM(keep.shape, jnp.bfloat16),
        compiler_params=pltpu.CompilerParams(vmem_limit_bytes=VMEM_LIMIT),
        name="early",
    )(bias.reshape(1, -1), keep, recv, *after)


def finish_kernel(tiles, chunks, live_ref, bias_ref, *refs):
    out, refs = refs[-1], list(refs[:-1])
    for phase, first, columns, count in chunks:
        parts, refs = refs[:count], refs[count:]
        value = parts[0][...] if count == 1 else activate(bias_ref, first, *parts)
        for tile in range(tiles):
            rows = value[tile * PART:(tile + 1) * PART]
            rows = jnp.where(live_ref[tile] > 0, rows, jnp.zeros_like(rows))
            out[tile, phase, :, first:first + columns] = rows


def finish(live, bias, chunks, flows, tiles):
    width = bias.shape[0]
    chunks = [chunk + (len(flow),) for chunk, flow in zip(chunks, flows)]
    flat = [array for flow in flows for array in flow]
    inside = pl.BlockSpec(memory_space=pltpu.VMEM)
    out = pl.pallas_call(
        functools.partial(finish_kernel, tiles, chunks),
        in_specs=[pl.BlockSpec(memory_space=pltpu.SMEM), inside] + [inside] * len(flat),
        out_specs=inside,
        out_shape=jax.ShapeDtypeStruct((tiles, PHASES, PART, width), jnp.bfloat16),
        compiler_params=pltpu.CompilerParams(vmem_limit_bytes=VMEM_LIMIT),
        name="finish",
    )(live, bias.reshape(1, width), *flat)
    return out.reshape(tiles * TILE_ROWS, width)


def exchange(array, masks, peers):
    pairs = [(2 * d + core, 2 * (d ^ mask) + core) for core, mask in enumerate(masks) for d in range(peers)]
    return lax.ppermute(array, ("dp", "tensor"), pairs)


def accumulate_kernel(count, *refs):
    send_out, keep_out = refs[-2:]
    half = send_out.shape[0]
    start = 0
    for index in range(count):
        keep_ref, recv_ref = refs[2 * index], refs[2 * index + 1]
        at = slice(start, start + keep_ref.shape[1])
        start = at.stop
        summed = keep_ref[...].astype(jnp.float32) + recv_ref[...].astype(jnp.float32)
        send_out[:, at] = summed[:half].astype(jnp.bfloat16)
        keep_out[:, at] = summed[half:]


def accumulate(flows, after):
    rows = flows[0][0].shape[0] // 2
    columns = sum(keep.shape[1] for keep, _ in flows)
    inside, outside = pl.BlockSpec(memory_space=pltpu.VMEM), pl.BlockSpec(memory_space=pl.ANY)
    return pl.pallas_call(
        functools.partial(accumulate_kernel, len(flows)),
        in_specs=[inside] * (2 * len(flows)) + [outside] * len(after),
        out_specs=[inside, inside],
        out_shape=[pltpu.VMEM((rows, columns), jnp.bfloat16), pltpu.VMEM((rows, columns), jnp.float32)],
        compiler_params=pltpu.CompilerParams(vmem_limit_bytes=VMEM_LIMIT),
        name="accumulate",
    )(*[array for flow in flows for array in flow], *after)


def body(patch_feats, ln_gain, ln_shift, merge_weight, merge_bias, tile_count, tile_dest):
    peers = lax.axis_size("dp")
    me = lax.axis_index("dp").astype(jnp.int32)
    tiles = patch_feats.shape[0] // TILE
    slots = peers * tiles
    bits = list(range(peers.bit_length() - 1))
    columns = merge_weight.shape[1]

    source_ids = jnp.arange(peers, dtype=jnp.int32)
    y_first, z_first = bits, [bits[1], bits[0]] + bits[2:]
    is_first = lax.axis_index("tensor") == 0
    tile_ids = jnp.arange(slots, dtype=jnp.int32)
    sent = jnp.array(sum(routes(peers), []), jnp.int32)
    all_sequences, orders = [(y_first, z_first), (y_first, z_first)], []
    for sequences in all_sequences:
        owners = [jnp.array(arrangement(sequence), jnp.int32) for sequence in sequences]
        owners = jnp.where(is_first, *owners) ^ me
        wanted = (owners[:, None] * tiles + jnp.arange(tiles, dtype=jnp.int32)[None, :]).reshape(slots)
        anchor = jnp.sum(jnp.where(tile_dest[None, :] == wanted[:, None], tile_ids[None, :], 0), axis=1)
        source, place = anchor // tiles, anchor % tiles
        is_there = sent[None, :] == (source ^ me)[:, None]
        orders.append(jnp.sum(jnp.where(is_there, source_ids[None, :], 0), axis=1) * tiles + place)
    own_source, own_place = source[-tiles:], place[-tiles:]
    own_count = jnp.sum(jnp.where(own_source[:, None] == source_ids[None, :], tile_count[None, :], 0), axis=1)
    live = (own_place < own_count).astype(jnp.int32)

    half = columns // 2
    chunks = [(0, 0, columns), (1, 0, half), (1, half, half)]
    pieces = [prepare(tile_count, patch_feats, ln_gain, ln_shift, peers, tiles, 0, [], [])]
    pieces.append(prepare(tile_count, patch_feats, ln_gain, ln_shift, peers, tiles, 1, pieces[0][-1:], pieces[0][:1]))
    received = [[send_piece(piece, i, peers) for i, piece in enumerate(parts[:-1])] for parts in pieces]
    last = send_piece(pieces[1][-1], peers // 2 - 1, peers)
    packed = {}

    flows, done, after = {}, {}, []
    steps = STEPS
    if len(bits) != 3:
        steps = [(index, step) for step in range(len(bits)) for index in range(len(chunks))]
    for index, step in steps:
        phase, first, count = chunks[index]
        if step < 0 or (step == 0 and first == 0 and phase not in packed):
            mine = pack(received[phase], last, pieces[1][-1], phase, after)
            packed[phase] = mine, lax.ppermute(mine, "tensor", [(0, 1), (1, 0)])
            after = [mine]
            if phase == 0:
                weight = load(merge_weight, after)
            if step < 0:
                continue
        if step == len(bits):
            done[index] = early(merge_bias, first, *flows[index], after)
            after = [done[index]]
            continue
        if step > 0:
            send, keep = accumulate([flows[index]], after)
        elif first == 0:
            rows, send, keep = gather_and_project(orders[phase], *packed[phase], weight, first, count, [], after)
        else:
            send, keep = project(rows, weight, first, count, after)
        after = [keep]
        flows[index] = (keep, exchange(send, [1 << sequence[step] for sequence in all_sequences[phase]], peers))
    flows = [(done[i],) if i in done else flows[i] for i in range(len(chunks))]
    return finish(live, merge_bias, chunks, flows, tiles)


def solution(mesh):
    in_specs = (
        P(("group", "dp"), None),
        P(),
        P(),
        P("dp", "tensor"),
        P("tensor"),
        P("group"),
        P("group"),
    )
    out_specs = P(("group", "dp"), "tensor")
    return jax.shard_map(body, mesh=mesh, in_specs=in_specs, out_specs=out_specs, check_vma=False)
```

```python
import functools
import math

import jax
import jax.numpy as jnp
from jax import lax
from jax.experimental import pallas as pl
from jax.experimental.pallas import tpu as pltpu
from jax.sharding import PartitionSpec as P

TILE = 128
TILE_ROWS = TILE // 4
PHASES = 2
PART = TILE_ROWS // PHASES
VMEM_LIMIT = 16 * 1024 * 1024
BIG_VMEM = 20 * 1024 * 1024
PROJECT_VMEM = 20 * 1024 * 1024
LANES = 128
STEPS = [(0, 0), (1, -1), (1, 0), (0, 1), (2, 0), (1, 1), (0, 2), (2, 1), (1, 2), (0, 3), (2, 2)]


def arrangement(bits):
    if not bits:
        return [0]
    rest = arrangement(bits[1:])
    return [owner ^ (1 << bits[0]) for owner in rest] + rest


def in_hbm(array):
    return pltpu.with_memory_space_constraint(array, pltpu.HBM)


def routes(peers):
    if peers == 8:
        return [[2, 4, 5, 1], [3, 6, 7, 0]]
    order = list(reversed(range(peers)))
    return [order[0::2], order[1::2]]


def prepare_kernel(peers, tiles, phase, x_hbm, gain_hbm, shift_hbm, count_hbm, *refs):
    outs, (pieces, x_ref, gain_ref, shift_ref, count_ref, sems) = refs[-6 - peers // 2:-6], refs[-6:]
    if phase == 1:
        outs[-1][:tiles * PART, :] = refs[0][...]
    me, core = lax.axis_index("dp"), lax.axis_index("tensor")
    width = x_hbm.shape[-1]
    total = 4 * width
    block_width = total // peers
    per_patch = width // block_width
    rows = tiles * PART
    copies = [
        pltpu.make_async_copy(x_hbm.at[:, phase], x_ref, sems.at[0]),
        pltpu.make_async_copy(gain_hbm, gain_ref, sems.at[1]),
        pltpu.make_async_copy(shift_hbm, shift_ref, sems.at[2]),
        pltpu.make_async_copy(count_hbm, count_ref, sems.at[3]),
    ]
    for copy in copies:
        copy.start()
    row_out = lax.broadcasted_iota(jnp.int32, (4 * rows, 4 * rows), 0)
    row_in = lax.broadcasted_iota(jnp.int32, (4 * rows, 4 * rows), 1)
    quarter = sum((row_out >= q * rows).astype(jnp.int32) for q in range(1, 4))
    source = 4 * (row_out - quarter * rows) + quarter
    mix = (row_in == source).astype(jnp.bfloat16)
    tile_of = lax.broadcasted_iota(jnp.int32, (rows, 1), 0) // PART
    for copy in copies:
        copy.wait()
    live = tile_of < count_ref[me]
    x = x_ref[...].reshape(4 * rows, width)
    y = jnp.dot(mix, x, preferred_element_type=jnp.float32)
    parts = [y[q * rows:(q + 1) * rows] for q in range(4)]
    mean = sum(jnp.sum(part, axis=1, keepdims=True) for part in parts) / total
    parts = [part - mean for part in parts]
    variance = sum(jnp.sum(part * part, axis=1, keepdims=True) for part in parts) / total
    scale = lax.rsqrt(variance + 1e-06)
    for q in range(4):
        normed = []
        for lane in range(width // LANES):
            at = pl.ds(q * (width // LANES) + lane, 1)
            part = parts[q][:, lane * LANES:(lane + 1) * LANES]
            normed.append(part * scale * gain_ref[at, :] + shift_ref[at, :])
        normed = jnp.concatenate(normed, axis=1)
        normed = jnp.where(live, normed, 0.0).astype(jnp.bfloat16)
        for part in range(per_patch):
            pieces[q * per_patch + part] = normed[:, part * block_width:(part + 1) * block_width]
    for out, first, second in zip(outs, *routes(peers)):
        value = pieces[jnp.bitwise_xor(me, jnp.where(core == 0, first, second))]
        out[out.shape[0] - tiles * PART:, :] = value


def prepare(tile_count, patch_feats, ln_gain, ln_shift, peers, tiles, phase, last, after):
    width = patch_feats.shape[1]
    block_width = 4 * width // peers
    rows = tiles * PART
    x = patch_feats.reshape(tiles, PHASES, 4 * PART, width)
    vectors = (4 * width // LANES, LANES)
    inside = pl.BlockSpec(memory_space=pltpu.VMEM)
    operands = [x, ln_gain.reshape(vectors), ln_shift.reshape(vectors), tile_count]
    return pl.pallas_call(
        functools.partial(prepare_kernel, peers, tiles, phase),
        in_specs=[pl.BlockSpec(memory_space=pl.ANY)] * 4 + [inside] * len(last) + [pl.BlockSpec(memory_space=pl.ANY)] * len(after),
        out_specs=[inside] * (peers // 2),
        scratch_shapes=[
            pltpu.VMEM((peers, rows, block_width), jnp.bfloat16),
            pltpu.VMEM((tiles, 4 * PART, width), jnp.bfloat16),
            pltpu.VMEM(vectors, jnp.float32),
            pltpu.VMEM(vectors, jnp.float32),
            pltpu.SMEM(tile_count.shape, jnp.int32),
            pltpu.SemaphoreType.DMA((4,)),
        ],
        out_shape=[pltpu.VMEM((rows, block_width), jnp.bfloat16)] * (peers // 2 - 1)
        + [pltpu.VMEM(((1 + len(last)) * rows, block_width), jnp.bfloat16)],
        compiler_params=pltpu.CompilerParams(vmem_limit_bytes=BIG_VMEM),
        cost_estimate=pl.CostEstimate(flops=0, bytes_accessed=32 * rows * width, transcendentals=0),
        name="prepare",
    )(*[in_hbm(operand) for operand in operands], *last, *after)


def send_piece(piece, index, peers):
    first, second = (route[index] for route in routes(peers))
    pairs = [(2 * d, 2 * (d ^ first)) for d in range(peers)]
    pairs += [(2 * d + 1, 2 * (d ^ second) + 1) for d in range(peers) if second != 0]
    return lax.ppermute(piece, ("dp", "tensor"), pairs)


def pack_kernel(count, phase, *refs):
    pieces, last, own, out = refs[:count], refs[count], refs[count + 1], refs[-1]
    rows, width = pieces[0].shape
    if out.shape[1] > width:
        out[:, width:] = jnp.zeros((out.shape[0], out.shape[1] - width), out.dtype)
    for i, piece in enumerate(pieces):
        out[i * rows:(i + 1) * rows, :width] = piece[...]
    at = slice(phase * rows, (phase + 1) * rows)
    out[count * rows:, :width] = jnp.where(lax.axis_index("tensor") == 0, last[at, :], own[at, :])


def pack(received, last, own, phase, after):
    rows, width = received[0].shape
    padded = -(-width // LANES) * LANES
    inside = pl.BlockSpec(memory_space=pltpu.VMEM)
    return pl.pallas_call(
        functools.partial(pack_kernel, len(received), phase),
        in_specs=[inside] * (len(received) + 2) + [pl.BlockSpec(memory_space=pl.ANY)] * len(after),
        out_specs=inside,
        out_shape=pltpu.VMEM(((len(received) + 1) * rows, padded), jnp.bfloat16),
        compiler_params=pltpu.CompilerParams(vmem_limit_bytes=VMEM_LIMIT),
        name="pack",
    )(*received, last, own, *after)


def load_kernel(w_hbm, piece_ref, w_ref, out_ref, sem):
    copy = pltpu.make_async_copy(w_hbm, w_ref, sem)
    copy.start()
    out_ref[...] = piece_ref[...]
    copy.wait()


def load(array, piece):
    inside = pl.BlockSpec(memory_space=pltpu.VMEM)
    return pl.pallas_call(
        load_kernel,
        in_specs=[pl.BlockSpec(memory_space=pl.ANY), inside],
        out_specs=[inside, inside],
        out_shape=[pltpu.VMEM(array.shape, array.dtype), pltpu.VMEM(piece.shape, piece.dtype)],
        scratch_shapes=[pltpu.SemaphoreType.DMA],
        compiler_params=pltpu.CompilerParams(vmem_limit_bytes=VMEM_LIMIT),
        cost_estimate=pl.CostEstimate(flops=0, bytes_accessed=4 * array.size, transcendentals=0),
        name="load",
    )(in_hbm(array), piece)


def multiply(first, block, a_ref, w_ref, send_ref, keep_ref):
    half = a_ref.shape[0] // 2
    for column in range(0, send_ref.shape[1], block):
        w = w_ref[:, first + column:first + column + block]
        acc = jnp.dot(a_ref[:, :w.shape[0]], w, preferred_element_type=jnp.float32)
        acc = acc.astype(jnp.bfloat16)
        send_ref[:, column:column + block] = acc[:half]
        keep_ref[:, column:column + block] = acc[half:]


def project_kernel(first, block, a_ref, w_ref, *refs):
    multiply(first, block, a_ref, w_ref, *refs[-2:])


def gather_kernel(first, block, count, order_ref, mine_ref, other_ref, w_ref, *refs):
    sorted_ref, send_ref, keep_ref = refs[-4 - count:-1 - count]
    held = refs[-1]
    for piece, out in zip(refs[:count], refs[-1 - count:-1]):
        out[...] = piece[...]
    core = lax.axis_index("tensor")
    held[core] = mine_ref[...]
    held[1 - core] = other_ref[...]
    half = mine_ref.shape[0] // PART
    for i in range(sorted_ref.shape[0] // PART):
        place = order_ref[i]
        side = (place >= half).astype(jnp.int32)
        start = pl.multiple_of((place - side * half) * PART, PART)
        sorted_ref[pl.ds(i * PART, PART), :] = held[side, pl.ds(start, PART), :]
    multiply(first, block, sorted_ref, w_ref, send_ref, keep_ref)


def cost(rows, depth, columns):
    return pl.CostEstimate(
        flops=2 * rows * depth * columns,
        bytes_accessed=2 * (rows * depth + depth * columns + rows * columns),
        transcendentals=0,
    )


def project(a, weight, first, columns, after, block=256):
    rows = a.shape[0]
    depth = weight.shape[0]
    half = pltpu.VMEM((rows // 2, columns), jnp.bfloat16)
    inside, outside = pl.BlockSpec(memory_space=pltpu.VMEM), pl.BlockSpec(memory_space=pl.ANY)
    return pl.pallas_call(
        functools.partial(project_kernel, first, block),
        in_specs=[inside] * 2 + [outside] * len(after),
        out_specs=[inside] * 2,
        out_shape=[half, half],
        compiler_params=pltpu.CompilerParams(vmem_limit_bytes=PROJECT_VMEM),
        cost_estimate=cost(rows, depth, columns),
        name="project",
    )(a, weight, *after)


def gather_and_project(order, mine, other, weight, first, columns, pieces, after, block=256):
    rows, padded = mine.shape
    depth = weight.shape[0]
    half = pltpu.VMEM((rows, columns), jnp.bfloat16)
    inside, outside = pl.BlockSpec(memory_space=pltpu.VMEM), pl.BlockSpec(memory_space=pl.ANY)
    return pl.pallas_call(
        functools.partial(gather_kernel, first, block, len(pieces)),
        in_specs=[pl.BlockSpec(memory_space=pltpu.SMEM)] + [inside] * (3 + len(pieces)) + [outside] * len(after),
        out_specs=[inside] * (3 + len(pieces)),
        out_shape=[pltpu.VMEM((2 * rows, padded), jnp.bfloat16), half, half]
        + [pltpu.VMEM(piece.shape, piece.dtype) for piece in pieces],
        scratch_shapes=[pltpu.VMEM((2, rows, padded), jnp.bfloat16)],
        compiler_params=pltpu.CompilerParams(vmem_limit_bytes=PROJECT_VMEM),
        cost_estimate=cost(2 * rows, depth, columns),
        name="gather_and_project",
    )(order, mine, other, weight, *pieces, *after)


def activate(bias_ref, first, keep_ref, recv_ref):
    summed = keep_ref[...].astype(jnp.float32) + recv_ref[...].astype(jnp.float32)
    summed += bias_ref[:, first:first + summed.shape[1]]
    return (0.5 * summed * (1.0 + lax.erf(summed * 0.7071067811865476))).astype(jnp.bfloat16)


def early_kernel(first, bias_ref, keep_ref, recv_ref, *refs):
    refs[-1][...] = activate(bias_ref, first, keep_ref, recv_ref)


def early(bias, first, keep, recv, after):
    inside, outside = pl.BlockSpec(memory_space=pltpu.VMEM), pl.BlockSpec(memory_space=pl.ANY)
    return pl.pallas_call(
        functools.partial(early_kernel, first),
        in_specs=[inside] * 3 + [outside] * len(after),
        out_specs=inside,
        out_shape=pltpu.VMEM(keep.shape, jnp.bfloat16),
        compiler_params=pltpu.CompilerParams(vmem_limit_bytes=VMEM_LIMIT),
        name="early",
    )(bias.reshape(1, -1), keep, recv, *after)


def finish_kernel(tiles, chunks, live_ref, bias_ref, *refs):
    out, refs = refs[-1], list(refs[:-1])
    for phase, first, columns, count in chunks:
        parts, refs = refs[:count], refs[count:]
        value = parts[0][...] if count == 1 else activate(bias_ref, first, *parts)
        for tile in range(tiles):
            rows = value[tile * PART:(tile + 1) * PART]
            rows = jnp.where(live_ref[tile] > 0, rows, jnp.zeros_like(rows))
            out[tile, phase, :, first:first + columns] = rows


def finish(live, bias, chunks, flows, tiles):
    width = bias.shape[0]
    chunks = [chunk + (len(flow),) for chunk, flow in zip(chunks, flows)]
    flat = [array for flow in flows for array in flow]
    inside = pl.BlockSpec(memory_space=pltpu.VMEM)
    out = pl.pallas_call(
        functools.partial(finish_kernel, tiles, chunks),
        in_specs=[pl.BlockSpec(memory_space=pltpu.SMEM), inside] + [inside] * len(flat),
        out_specs=inside,
        out_shape=jax.ShapeDtypeStruct((tiles, PHASES, PART, width), jnp.bfloat16),
        compiler_params=pltpu.CompilerParams(vmem_limit_bytes=VMEM_LIMIT),
        name="finish",
    )(live, bias.reshape(1, width), *flat)
    return out.reshape(tiles * TILE_ROWS, width)


def exchange(array, masks, peers):
    pairs = [(2 * d + core, 2 * (d ^ mask) + core) for core, mask in enumerate(masks) for d in range(peers)]
    return lax.ppermute(array, ("dp", "tensor"), pairs)


def accumulate_kernel(count, *refs):
    send_out, keep_out = refs[-2:]
    half = send_out.shape[0]
    start = 0
    for index in range(count):
        keep_ref, recv_ref = refs[2 * index], refs[2 * index + 1]
        at = slice(start, start + keep_ref.shape[1])
        start = at.stop
        summed = keep_ref[...].astype(jnp.float32) + recv_ref[...].astype(jnp.float32)
        send_out[:, at] = summed[:half].astype(jnp.bfloat16)
        keep_out[:, at] = summed[half:]


def accumulate(flows, after):
    rows = flows[0][0].shape[0] // 2
    columns = sum(keep.shape[1] for keep, _ in flows)
    inside, outside = pl.BlockSpec(memory_space=pltpu.VMEM), pl.BlockSpec(memory_space=pl.ANY)
    return pl.pallas_call(
        functools.partial(accumulate_kernel, len(flows)),
        in_specs=[inside] * (2 * len(flows)) + [outside] * len(after),
        out_specs=[inside, inside],
        out_shape=[pltpu.VMEM((rows, columns), jnp.bfloat16), pltpu.VMEM((rows, columns), jnp.float32)],
        compiler_params=pltpu.CompilerParams(vmem_limit_bytes=VMEM_LIMIT),
        name="accumulate",
    )(*[array for flow in flows for array in flow], *after)


def body(patch_feats, ln_gain, ln_shift, merge_weight, merge_bias, tile_count, tile_dest):
    peers = lax.axis_size("dp")
    me = lax.axis_index("dp").astype(jnp.int32)
    tiles = patch_feats.shape[0] // TILE
    slots = peers * tiles
    bits = list(range(peers.bit_length() - 1))
    columns = merge_weight.shape[1]

    source_ids = jnp.arange(peers, dtype=jnp.int32)
    y_first, z_first = bits, [bits[1], bits[0]] + bits[2:]
    is_first = lax.axis_index("tensor") == 0
    tile_ids = jnp.arange(slots, dtype=jnp.int32)
    sent = jnp.array(sum(routes(peers), []), jnp.int32)
    all_sequences, orders = [(y_first, z_first), (y_first, z_first)], []
    for sequences in all_sequences:
        owners = [jnp.array(arrangement(sequence), jnp.int32) for sequence in sequences]
        owners = jnp.where(is_first, *owners) ^ me
        wanted = (owners[:, None] * tiles + jnp.arange(tiles, dtype=jnp.int32)[None, :]).reshape(slots)
        anchor = jnp.sum(jnp.where(tile_dest[None, :] == wanted[:, None], tile_ids[None, :], 0), axis=1)
        source, place = anchor // tiles, anchor % tiles
        is_there = sent[None, :] == (source ^ me)[:, None]
        orders.append(jnp.sum(jnp.where(is_there, source_ids[None, :], 0), axis=1) * tiles + place)
    own_source, own_place = source[-tiles:], place[-tiles:]
    own_count = jnp.sum(jnp.where(own_source[:, None] == source_ids[None, :], tile_count[None, :], 0), axis=1)
    live = (own_place < own_count).astype(jnp.int32)

    half = columns // 2
    chunks = [(0, 0, columns), (1, 0, half), (1, half, half)]
    pieces = [prepare(tile_count, patch_feats, ln_gain, ln_shift, peers, tiles, 0, [], [])]
    pieces.append(prepare(tile_count, patch_feats, ln_gain, ln_shift, peers, tiles, 1, pieces[0][-1:], pieces[0][:1]))
    pieces[1] = list(pieces[1])
    weight, pieces[1][-2] = load(merge_weight, pieces[1][-2])
    received = [[send_piece(piece, i, peers) for i, piece in enumerate(parts[:-1])] for parts in pieces]
    last = send_piece(pieces[1][-1], peers // 2 - 1, peers)
    packed = {}

    flows, done, after = {}, {}, []
    steps = STEPS
    if len(bits) != 3:
        steps = [(index, step) for step in range(len(bits)) for index in range(len(chunks))]
    for index, step in steps:
        phase, first, count = chunks[index]
        if step < 0 or (step == 0 and first == 0 and phase not in packed):
            mine = pack(received[phase], last, pieces[1][-1], phase, after)
            packed[phase] = mine, lax.ppermute(mine, "tensor", [(0, 1), (1, 0)])
            after = [mine]
            if step < 0:
                continue
        if step == len(bits):
            done[index] = early(merge_bias, first, *flows[index], after)
            after = [done[index]]
            continue
        if step > 0:
            send, keep = accumulate([flows[index]], after)
        elif first == 0:
            rows, send, keep = gather_and_project(orders[phase], *packed[phase], weight, first, count, [], after)
        else:
            send, keep = project(rows, weight, first, count, after)
        after = [keep]
        flows[index] = (keep, exchange(send, [1 << sequence[step] for sequence in all_sequences[phase]], peers))
    flows = [(done[i],) if i in done else flows[i] for i in range(len(chunks))]
    return finish(live, merge_bias, chunks, flows, tiles)


def solution(mesh):
    in_specs = (
        P(("group", "dp"), None),
        P(),
        P(),
        P("dp", "tensor"),
        P("tensor"),
        P("group"),
        P("group"),
    )
    out_specs = P(("group", "dp"), "tensor")
    return jax.shard_map(body, mesh=mesh, in_specs=in_specs, out_specs=out_specs, check_vma=False)
```

```python
import functools
import math

import jax
import jax.numpy as jnp
from jax import lax
from jax.experimental import pallas as pl
from jax.experimental.pallas import tpu as pltpu
from jax.sharding import PartitionSpec as P

TILE = 128
TILE_ROWS = TILE // 4
PHASES = 2
PART = TILE_ROWS // PHASES
VMEM_LIMIT = 16 * 1024 * 1024
BIG_VMEM = 20 * 1024 * 1024
PROJECT_VMEM = 20 * 1024 * 1024
LANES = 128
STEPS = [(0, 0), (1, -1), (1, 0), (0, 1), (2, 0), (1, 1), (0, 2), (2, 1), (1, 2), (0, 3), (2, 2)]


def arrangement(bits):
    if not bits:
        return [0]
    rest = arrangement(bits[1:])
    return [owner ^ (1 << bits[0]) for owner in rest] + rest


def in_hbm(array):
    return pltpu.with_memory_space_constraint(array, pltpu.HBM)


def routes(peers):
    if peers == 8:
        return [[2, 4, 5, 1], [3, 6, 7, 0]]
    order = list(reversed(range(peers)))
    return [order[0::2], order[1::2]]


def prepare_kernel(peers, tiles, phase, x_hbm, gain_hbm, shift_hbm, count_hbm, *refs):
    outs, (pieces, x_ref, gain_ref, shift_ref, count_ref, sems) = refs[-6 - peers // 2:-6], refs[-6:]
    if phase == 1:
        outs[-1][:tiles * PART, :] = refs[0][...]
    me, core = lax.axis_index("dp"), lax.axis_index("tensor")
    width = x_hbm.shape[-1]
    total = 4 * width
    block_width = total // peers
    per_patch = width // block_width
    rows = tiles * PART
    copies = [
        pltpu.make_async_copy(x_hbm.at[:, phase], x_ref, sems.at[0]),
        pltpu.make_async_copy(gain_hbm, gain_ref, sems.at[1]),
        pltpu.make_async_copy(shift_hbm, shift_ref, sems.at[2]),
        pltpu.make_async_copy(count_hbm, count_ref, sems.at[3]),
    ]
    for copy in copies:
        copy.start()
    row_out = lax.broadcasted_iota(jnp.int32, (4 * rows, 4 * rows), 0)
    row_in = lax.broadcasted_iota(jnp.int32, (4 * rows, 4 * rows), 1)
    quarter = sum((row_out >= q * rows).astype(jnp.int32) for q in range(1, 4))
    source = 4 * (row_out - quarter * rows) + quarter
    mix = (row_in == source).astype(jnp.bfloat16)
    tile_of = lax.broadcasted_iota(jnp.int32, (rows, 1), 0) // PART
    for copy in copies:
        copy.wait()
    live = tile_of < count_ref[me]
    x = x_ref[...].reshape(4 * rows, width)
    y = jnp.dot(mix, x, preferred_element_type=jnp.float32)
    parts = [y[q * rows:(q + 1) * rows] for q in range(4)]
    mean = sum(jnp.sum(part, axis=1, keepdims=True) for part in parts) / total
    parts = [part - mean for part in parts]
    variance = sum(jnp.sum(part * part, axis=1, keepdims=True) for part in parts) / total
    scale = lax.rsqrt(variance + 1e-06)
    for q in range(4):
        normed = []
        for lane in range(width // LANES):
            at = pl.ds(q * (width // LANES) + lane, 1)
            part = parts[q][:, lane * LANES:(lane + 1) * LANES]
            normed.append(part * scale * gain_ref[at, :] + shift_ref[at, :])
        normed = jnp.concatenate(normed, axis=1)
        normed = jnp.where(live, normed, 0.0).astype(jnp.bfloat16)
        for part in range(per_patch):
            pieces[q * per_patch + part] = normed[:, part * block_width:(part + 1) * block_width]
    for out, first, second in zip(outs, *routes(peers)):
        value = pieces[jnp.bitwise_xor(me, jnp.where(core == 0, first, second))]
        out[out.shape[0] - tiles * PART:, :] = value


def prepare(tile_count, patch_feats, ln_gain, ln_shift, peers, tiles, phase, last, after):
    width = patch_feats.shape[1]
    block_width = 4 * width // peers
    rows = tiles * PART
    x = patch_feats.reshape(tiles, PHASES, 4 * PART, width)
    vectors = (4 * width // LANES, LANES)
    inside = pl.BlockSpec(memory_space=pltpu.VMEM)
    operands = [x, ln_gain.reshape(vectors), ln_shift.reshape(vectors), tile_count]
    return pl.pallas_call(
        functools.partial(prepare_kernel, peers, tiles, phase),
        in_specs=[pl.BlockSpec(memory_space=pl.ANY)] * 4 + [inside] * len(last) + [pl.BlockSpec(memory_space=pl.ANY)] * len(after),
        out_specs=[inside] * (peers // 2),
        scratch_shapes=[
            pltpu.VMEM((peers, rows, block_width), jnp.bfloat16),
            pltpu.VMEM((tiles, 4 * PART, width), jnp.bfloat16),
            pltpu.VMEM(vectors, jnp.float32),
            pltpu.VMEM(vectors, jnp.float32),
            pltpu.SMEM(tile_count.shape, jnp.int32),
            pltpu.SemaphoreType.DMA((4,)),
        ],
        out_shape=[pltpu.VMEM((rows, block_width), jnp.bfloat16)] * (peers // 2 - 1)
        + [pltpu.VMEM(((1 + len(last)) * rows, block_width), jnp.bfloat16)],
        compiler_params=pltpu.CompilerParams(vmem_limit_bytes=BIG_VMEM),
        cost_estimate=pl.CostEstimate(flops=0, bytes_accessed=32 * rows * width, transcendentals=0),
        name="prepare",
    )(*[in_hbm(operand) for operand in operands], *last, *after)


def send_piece(piece, index, peers):
    first, second = (route[index] for route in routes(peers))
    pairs = [(2 * d, 2 * (d ^ first)) for d in range(peers)]
    pairs += [(2 * d + 1, 2 * (d ^ second) + 1) for d in range(peers) if second != 0]
    return lax.ppermute(piece, ("dp", "tensor"), pairs)


def pack_kernel(count, phase, *refs):
    pieces, last, own, out = refs[:count], refs[count], refs[count + 1], refs[-1]
    rows, width = pieces[0].shape
    if out.shape[1] > width:
        out[:, width:] = jnp.zeros((out.shape[0], out.shape[1] - width), out.dtype)
    for i, piece in enumerate(pieces):
        out[i * rows:(i + 1) * rows, :width] = piece[...]
    at = slice(phase * rows, (phase + 1) * rows)
    out[count * rows:, :width] = jnp.where(lax.axis_index("tensor") == 0, last[at, :], own[at, :])


def pack(received, last, own, phase, after):
    rows, width = received[0].shape
    padded = -(-width // LANES) * LANES
    inside = pl.BlockSpec(memory_space=pltpu.VMEM)
    return pl.pallas_call(
        functools.partial(pack_kernel, len(received), phase),
        in_specs=[inside] * (len(received) + 2) + [pl.BlockSpec(memory_space=pl.ANY)] * len(after),
        out_specs=inside,
        out_shape=pltpu.VMEM(((len(received) + 1) * rows, padded), jnp.bfloat16),
        compiler_params=pltpu.CompilerParams(vmem_limit_bytes=VMEM_LIMIT),
        name="pack",
    )(*received, last, own, *after)


def load_kernel(w_hbm, piece_ref, w_ref, out_ref, sem):
    copy = pltpu.make_async_copy(w_hbm, w_ref, sem)
    copy.start()
    out_ref[...] = piece_ref[...]
    copy.wait()


def load(array, piece):
    inside = pl.BlockSpec(memory_space=pltpu.VMEM)
    return pl.pallas_call(
        load_kernel,
        in_specs=[pl.BlockSpec(memory_space=pl.ANY), inside],
        out_specs=[inside, inside],
        out_shape=[pltpu.VMEM(array.shape, array.dtype), pltpu.VMEM(piece.shape, piece.dtype)],
        scratch_shapes=[pltpu.SemaphoreType.DMA],
        compiler_params=pltpu.CompilerParams(vmem_limit_bytes=VMEM_LIMIT),
        cost_estimate=pl.CostEstimate(flops=0, bytes_accessed=4 * array.size, transcendentals=0),
        name="load",
    )(in_hbm(array), piece)


def multiply(first, block, a_ref, w_ref, send_ref, keep_ref):
    half = a_ref.shape[0] // 2
    for column in range(0, send_ref.shape[1], block):
        w = w_ref[:, first + column:first + column + block]
        acc = jnp.dot(a_ref[:, :w.shape[0]], w, preferred_element_type=jnp.float32)
        acc = acc.astype(jnp.bfloat16)
        send_ref[:, column:column + block] = acc[:half]
        keep_ref[:, column:column + block] = acc[half:]


def project_kernel(first, block, a_ref, w_ref, *refs):
    multiply(first, block, a_ref, w_ref, *refs[-2:])


def gather_kernel(first, block, count, order_ref, mine_ref, other_ref, w_ref, *refs):
    sorted_ref, send_ref, keep_ref = refs[-4 - count:-1 - count]
    held = refs[-1]
    for piece, out in zip(refs[:count], refs[-1 - count:-1]):
        out[...] = piece[...]
    core = lax.axis_index("tensor")
    half = mine_ref.shape[0] // PART
    for i in range(sorted_ref.shape[0] // PART):
        place = order_ref[i]
        side = (place >= half).astype(jnp.int32)
        start = pl.multiple_of((place - side * half) * PART, PART)
        tile = jnp.where(side == core, mine_ref[pl.ds(start, PART), :], other_ref[pl.ds(start, PART), :])
        sorted_ref[pl.ds(i * PART, PART), :] = tile
    multiply(first, block, sorted_ref, w_ref, send_ref, keep_ref)


def cost(rows, depth, columns):
    return pl.CostEstimate(
        flops=2 * rows * depth * columns,
        bytes_accessed=2 * (rows * depth + depth * columns + rows * columns),
        transcendentals=0,
    )


def project(a, weight, first, columns, after, block=256):
    rows = a.shape[0]
    depth = weight.shape[0]
    half = pltpu.VMEM((rows // 2, columns), jnp.bfloat16)
    inside, outside = pl.BlockSpec(memory_space=pltpu.VMEM), pl.BlockSpec(memory_space=pl.ANY)
    return pl.pallas_call(
        functools.partial(project_kernel, first, block),
        in_specs=[inside] * 2 + [outside] * len(after),
        out_specs=[inside] * 2,
        out_shape=[half, half],
        compiler_params=pltpu.CompilerParams(vmem_limit_bytes=PROJECT_VMEM),
        cost_estimate=cost(rows, depth, columns),
        name="project",
    )(a, weight, *after)


def gather_and_project(order, mine, other, weight, first, columns, pieces, after, block=256):
    rows, padded = mine.shape
    depth = weight.shape[0]
    half = pltpu.VMEM((rows, columns), jnp.bfloat16)
    inside, outside = pl.BlockSpec(memory_space=pltpu.VMEM), pl.BlockSpec(memory_space=pl.ANY)
    return pl.pallas_call(
        functools.partial(gather_kernel, first, block, len(pieces)),
        in_specs=[pl.BlockSpec(memory_space=pltpu.SMEM)] + [inside] * (3 + len(pieces)) + [outside] * len(after),
        out_specs=[inside] * (3 + len(pieces)),
        out_shape=[pltpu.VMEM((2 * rows, padded), jnp.bfloat16), half, half]
        + [pltpu.VMEM(piece.shape, piece.dtype) for piece in pieces],
        scratch_shapes=[pltpu.VMEM((2, rows, padded), jnp.bfloat16)],
        compiler_params=pltpu.CompilerParams(vmem_limit_bytes=PROJECT_VMEM),
        cost_estimate=cost(2 * rows, depth, columns),
        name="gather_and_project",
    )(order, mine, other, weight, *pieces, *after)


def activate(bias_ref, first, keep_ref, recv_ref):
    summed = keep_ref[...].astype(jnp.float32) + recv_ref[...].astype(jnp.float32)
    summed += bias_ref[:, first:first + summed.shape[1]]
    return (0.5 * summed * (1.0 + lax.erf(summed * 0.7071067811865476))).astype(jnp.bfloat16)


def early_kernel(first, bias_ref, keep_ref, recv_ref, *refs):
    refs[-1][...] = activate(bias_ref, first, keep_ref, recv_ref)


def early(bias, first, keep, recv, after):
    inside, outside = pl.BlockSpec(memory_space=pltpu.VMEM), pl.BlockSpec(memory_space=pl.ANY)
    return pl.pallas_call(
        functools.partial(early_kernel, first),
        in_specs=[inside] * 3 + [outside] * len(after),
        out_specs=inside,
        out_shape=pltpu.VMEM(keep.shape, jnp.bfloat16),
        compiler_params=pltpu.CompilerParams(vmem_limit_bytes=VMEM_LIMIT),
        name="early",
    )(bias.reshape(1, -1), keep, recv, *after)


def finish_kernel(tiles, chunks, live_ref, bias_ref, *refs):
    out, refs = refs[-1], list(refs[:-1])
    for phase, first, columns, count in chunks:
        parts, refs = refs[:count], refs[count:]
        value = parts[0][...] if count == 1 else activate(bias_ref, first, *parts)
        for tile in range(tiles):
            rows = value[tile * PART:(tile + 1) * PART]
            rows = jnp.where(live_ref[tile] > 0, rows, jnp.zeros_like(rows))
            out[tile, phase, :, first:first + columns] = rows


def finish(live, bias, chunks, flows, tiles):
    width = bias.shape[0]
    chunks = [chunk + (len(flow),) for chunk, flow in zip(chunks, flows)]
    flat = [array for flow in flows for array in flow]
    inside = pl.BlockSpec(memory_space=pltpu.VMEM)
    out = pl.pallas_call(
        functools.partial(finish_kernel, tiles, chunks),
        in_specs=[pl.BlockSpec(memory_space=pltpu.SMEM), inside] + [inside] * len(flat),
        out_specs=inside,
        out_shape=jax.ShapeDtypeStruct((tiles, PHASES, PART, width), jnp.bfloat16),
        compiler_params=pltpu.CompilerParams(vmem_limit_bytes=VMEM_LIMIT),
        name="finish",
    )(live, bias.reshape(1, width), *flat)
    return out.reshape(tiles * TILE_ROWS, width)


def exchange(array, masks, peers):
    pairs = [(2 * d + core, 2 * (d ^ mask) + core) for core, mask in enumerate(masks) for d in range(peers)]
    return lax.ppermute(array, ("dp", "tensor"), pairs)


def accumulate_kernel(count, *refs):
    send_out, keep_out = refs[-2:]
    half = send_out.shape[0]
    start = 0
    for index in range(count):
        keep_ref, recv_ref = refs[2 * index], refs[2 * index + 1]
        at = slice(start, start + keep_ref.shape[1])
        start = at.stop
        summed = keep_ref[...].astype(jnp.float32) + recv_ref[...].astype(jnp.float32)
        send_out[:, at] = summed[:half].astype(jnp.bfloat16)
        keep_out[:, at] = summed[half:]


def accumulate(flows, after):
    rows = flows[0][0].shape[0] // 2
    columns = sum(keep.shape[1] for keep, _ in flows)
    inside, outside = pl.BlockSpec(memory_space=pltpu.VMEM), pl.BlockSpec(memory_space=pl.ANY)
    return pl.pallas_call(
        functools.partial(accumulate_kernel, len(flows)),
        in_specs=[inside] * (2 * len(flows)) + [outside] * len(after),
        out_specs=[inside, inside],
        out_shape=[pltpu.VMEM((rows, columns), jnp.bfloat16), pltpu.VMEM((rows, columns), jnp.float32)],
        compiler_params=pltpu.CompilerParams(vmem_limit_bytes=VMEM_LIMIT),
        name="accumulate",
    )(*[array for flow in flows for array in flow], *after)


def body(patch_feats, ln_gain, ln_shift, merge_weight, merge_bias, tile_count, tile_dest):
    peers = lax.axis_size("dp")
    me = lax.axis_index("dp").astype(jnp.int32)
    tiles = patch_feats.shape[0] // TILE
    slots = peers * tiles
    bits = list(range(peers.bit_length() - 1))
    columns = merge_weight.shape[1]

    source_ids = jnp.arange(peers, dtype=jnp.int32)
    y_first, z_first = bits, [bits[1], bits[0]] + bits[2:]
    is_first = lax.axis_index("tensor") == 0
    tile_ids = jnp.arange(slots, dtype=jnp.int32)
    sent = jnp.array(sum(routes(peers), []), jnp.int32)
    all_sequences, orders = [(y_first, z_first), (y_first, z_first)], []
    for sequences in all_sequences:
        owners = [jnp.array(arrangement(sequence), jnp.int32) for sequence in sequences]
        owners = jnp.where(is_first, *owners) ^ me
        wanted = (owners[:, None] * tiles + jnp.arange(tiles, dtype=jnp.int32)[None, :]).reshape(slots)
        anchor = jnp.sum(jnp.where(tile_dest[None, :] == wanted[:, None], tile_ids[None, :], 0), axis=1)
        source, place = anchor // tiles, anchor % tiles
        is_there = sent[None, :] == (source ^ me)[:, None]
        orders.append(jnp.sum(jnp.where(is_there, source_ids[None, :], 0), axis=1) * tiles + place)
    own_source, own_place = source[-tiles:], place[-tiles:]
    own_count = jnp.sum(jnp.where(own_source[:, None] == source_ids[None, :], tile_count[None, :], 0), axis=1)
    live = (own_place < own_count).astype(jnp.int32)

    half = columns // 2
    chunks = [(0, 0, columns), (1, 0, half), (1, half, half)]
    pieces = [prepare(tile_count, patch_feats, ln_gain, ln_shift, peers, tiles, 0, [], [])]
    pieces.append(prepare(tile_count, patch_feats, ln_gain, ln_shift, peers, tiles, 1, pieces[0][-1:], pieces[0][:1]))
    pieces[1] = list(pieces[1])
    weight, pieces[1][-2] = load(merge_weight, pieces[1][-2])
    received = [[send_piece(piece, i, peers) for i, piece in enumerate(parts[:-1])] for parts in pieces]
    last = send_piece(pieces[1][-1], peers // 2 - 1, peers)
    packed = {}

    flows, done, after = {}, {}, []
    steps = STEPS
    if len(bits) != 3:
        steps = [(index, step) for step in range(len(bits)) for index in range(len(chunks))]
    for index, step in steps:
        phase, first, count = chunks[index]
        if step < 0 or (step == 0 and first == 0 and phase not in packed):
            mine = pack(received[phase], last, pieces[1][-1], phase, after)
            packed[phase] = mine, lax.ppermute(mine, "tensor", [(0, 1), (1, 0)])
            after = [mine]
            if step < 0:
                continue
        if step == len(bits):
            done[index] = early(merge_bias, first, *flows[index], after)
            after = [done[index]]
            continue
        if step > 0:
            send, keep = accumulate([flows[index]], after)
        elif first == 0:
            rows, send, keep = gather_and_project(orders[phase], *packed[phase], weight, first, count, [], after)
        else:
            send, keep = project(rows, weight, first, count, after)
        after = [keep]
        flows[index] = (keep, exchange(send, [1 << sequence[step] for sequence in all_sequences[phase]], peers))
    flows = [(done[i],) if i in done else flows[i] for i in range(len(chunks))]
    return finish(live, merge_bias, chunks, flows, tiles)


def solution(mesh):
    in_specs = (
        P(("group", "dp"), None),
        P(),
        P(),
        P("dp", "tensor"),
        P("tensor"),
        P("group"),
        P("group"),
    )
    out_specs = P(("group", "dp"), "tensor")
    return jax.shard_map(body, mesh=mesh, in_specs=in_specs, out_specs=out_specs, check_vma=False)
```
